256 devices in a mesh: blk: 16 (over x, y_lo, core), uly: 16 (over z, y_hi).
Axes of the slice: x: 4, y: 4 (y_hi: 2, y_lo: 2; y = y_hi * 2 + y_lo), z: 8, core: 2. Of those that a mesh axis runs over, the one named last changes fastest.
Arguments:
- queries: bfloat16 [32768, 4096], P(('blk', 'uly')), may hold values from -128 to 128
- keys: bfloat16 [32768, 1024], P(('blk', 'uly')), may hold values from -7 to 7
- values: bfloat16 [32768, 1024], P(('blk', 'uly')), may hold values from -6 to 6
- doc_ids: int32 [32768], P(('blk', 'uly')), may hold values from 0 to 63, never falling along the last dimension, each value on 1 to 2048 neighbouring positions
- out_weight: bfloat16 [4096, 4096], P('uly'), may hold values from -0.09375 to 0.09375
Outputs:
- mixed: bfloat16 [32768, 4096], P(('blk', 'uly'))
The draws below stay inside these ranges and needn't reach their ends.
Inputs may be any that keep to these rules, and one draw needn't show every extreme that they name: `doc_ids`: document numbers never fall along the pack; each document holds 1 to 2048 consecutive tokens, and some document holds exactly 2048.
All inputs are finite; a program needn't handle non-finite values.
Results may differ from the reference program's by a relative error of at most 0.017.
Values may be sent and summed in bfloat16 or wider, within the bound.
No kernel may reach another device: no remote copies, remote signals or barrier semaphores. Data moves between devices by JAX's collectives and lax.ppermute only.
A program may use at most 64 MiB of HBM per device.

```python
import math
import jax
import jax.numpy as jnp
import numpy as np
from jax import lax

HEADS = 32
KV_HEADS = 8
HEAD_DIM = 128
OUT_COLS = 4096
Q_WIDTH = 4096
TOKENS = 32768
DOC_MOST = 2048
DOCS = 64
N_ULY = 16


def paired_draw(key):
    base = jax.random.fold_in(key, 4242)
    first, second = jax.random.split(base, 2)
    key_rows = jax.random.truncated_normal(first, -6.0, 6.0, (TOKENS, KV_HEADS * HEAD_DIM), jnp.float32)
    query_rows = jax.random.truncated_normal(second, -6.0, 6.0, (TOKENS, HEADS * HEAD_DIM), jnp.float32)
    return (query_rows, key_rows)


def draw_queries(key, part):
    return paired_draw(key)[0].astype(jnp.bfloat16)


def draw_keys(key, part):
    return paired_draw(key)[1].astype(jnp.bfloat16)


def steps_of(key, extent, cuts, least, largest):
    factor_of, own = 1.0, jax.random.fold_in(key, 6)
    for dim, shards_of in cuts:
        steps = jnp.exp(jax.random.uniform(jax.random.fold_in(own, dim), (shards_of,), jnp.float32, least / len(cuts), largest / len(cuts)))
        factor_of = factor_of * jnp.repeat(steps, extent[dim] // shards_of).reshape([-1 if axis == dim else 1 for axis in range(len(extent))])
    return factor_of


def length_profile(amount, total, bound, slope):
    weights = [(1 << 20) // math.isqrt(grade ** slope) + 1 for grade in range(2, amount + 1)]
    rest, given = total - bound - (amount - 1), [1] * (amount - 1)
    while rest > 0:
        movable = [i for i in range(amount - 1) if given[i] < bound]
        pool, budget = sum([weights[i] for i in movable]), rest
        for i in movable:
            extra = min(bound - given[i], max(1, budget * weights[i] // pool), rest)
            given[i] = given[i] + extra
            rest = rest - extra
    return np.array([bound] + given)


def uneven_parts(rng, number_of, total, bound, slope):
    if number_of == 2:
        one = jax.random.randint(rng, (), max(1, total - bound), min(bound, total - 1) + 1)
        return jnp.stack([one, total - one])
    tallies = jnp.asarray(length_profile(number_of, total, bound, slope), jnp.int32)
    twos = (number_of - 1) // 2
    giver, receiver = tallies[1:1 + 2 * twos:2], tallies[2:2 + 2 * twos:2]
    margin = jnp.minimum(giver - 1, bound - receiver)
    passed = jax.random.randint(jax.random.fold_in(rng, 1), (twos,), 0, 1 << 20) % (margin + 1)
    tallies = tallies.at[1:1 + 2 * twos:2].set(giver - passed).at[2:2 + 2 * twos:2].set(receiver + passed)
    return tallies[jax.random.permutation(jax.random.fold_in(rng, 2), number_of)]


def normal_values(rng, shape, scale, most, cuts=(), held_as=jnp.bfloat16):
    gain = steps_of(rng, shape, cuts, -0.22, 0.18) if cuts else 1.0
    values = jax.random.normal(rng, shape, jnp.float32) * scale * gain
    return jnp.minimum(jnp.maximum(values, -most), most).astype(held_as)


def setup_inputs(seed: int = 0) -> dict:
    splits = jax.random.split(jax.random.key(seed), 6)
    return {
        "queries": draw_queries(jax.random.fold_in(splits[5], 71), 0),
        "keys": draw_keys(jax.random.fold_in(splits[5], 71), 0),
        "values": normal_values(splits[2], (TOKENS, KV_HEADS * HEAD_DIM), 1.0, 6.0, ((0, 256),)),
        "doc_ids": jnp.searchsorted(jnp.cumsum(uneven_parts(splits[3], DOCS, TOKENS, DOC_MOST, 1)), jnp.arange(TOKENS), side="right").astype(jnp.int32),
        "out_weight": normal_values(splits[4], (Q_WIDTH, OUT_COLS), Q_WIDTH ** -0.5, 0.09375, ((0, 16),)),
    }


def attend_block(query_block, key_block, value_block, allowed, scale):
    scores = jnp.einsum("qgd,pd->gqp", query_block.astype(jnp.float32), key_block.astype(jnp.float32)) * scale
    scores = jnp.where(allowed[None], scores, -1e30)
    peak = jnp.max(scores, axis=-1, keepdims=True)
    expo = jnp.where(allowed[None], jnp.exp(scores - peak), 0.0)
    total = jnp.sum(expo, axis=-1)
    rounded = expo.astype(jnp.bfloat16).astype(jnp.float32)
    summed = jnp.einsum("gqp,pd->gqd", rounded, value_block.astype(jnp.float32))
    return (summed / total[..., None]).astype(jnp.bfloat16)


def reference(queries, keys, values, doc_ids, out_weight):
    qrows = min(TOKENS, 1024)
    group = HEADS // KV_HEADS
    scale = 1.0 / (HEAD_DIM ** 0.5)
    pieces = []
    for qstart in range(0, TOKENS, qrows):
        kstart = max(0, qstart - DOC_MOST)
        kend = qstart + qrows
        length = kend - kstart
        qpos = qstart + jnp.arange(qrows, dtype=jnp.int32)
        kpos = kstart + jnp.arange(length, dtype=jnp.int32)
        allowed = (kpos[None, :] <= qpos[:, None]) & (doc_ids[kstart:kend][None, :] == doc_ids[qstart:kend][:, None])
        query_block = queries[qstart:kend].reshape(qrows, KV_HEADS, group, HEAD_DIM).transpose(1, 0, 2, 3)
        key_block = keys[kstart:kend].reshape(length, KV_HEADS, HEAD_DIM).transpose(1, 0, 2)
        value_block = values[kstart:kend].reshape(length, KV_HEADS, HEAD_DIM).transpose(1, 0, 2)
        result = lax.map(lambda item: attend_block(item[0], item[1], item[2], allowed, scale), (query_block, key_block, value_block))
        pieces.append(result.transpose(2, 0, 1, 3).reshape(qrows, HEADS * HEAD_DIM))
    attn = jnp.concatenate(pieces, axis=0)
    share = (HEADS // N_ULY) * HEAD_DIM
    mixed = jnp.zeros((TOKENS, OUT_COLS), jnp.float32)
    for group_index in range(N_ULY):
        partial_value = jnp.dot(attn[:, group_index * share:(group_index + 1) * share], out_weight[group_index * share:(group_index + 1) * share], preferred_element_type=jnp.float32)
        partial_value = lax.optimization_barrier(partial_value.astype(jnp.bfloat16))
        mixed = mixed + partial_value.astype(jnp.float32)
    return mixed.astype(jnp.bfloat16)
```

```python
import functools
import math

import jax
import jax.numpy as jnp
from jax import lax
from jax.experimental import pallas as pl
from jax.experimental.pallas import tpu as pltpu
from jax.sharding import Mesh
from jax.sharding import PartitionSpec as P

HEAD_DIM = 128
ROWS = 128
Z = 8
GROUP = 4
PAIRS = 16
EXP2_SCALE = math.log2(math.e) / math.sqrt(HEAD_DIM)
MASKED = -1e30
VMEM_LIMIT = 48 * 1024 * 1024

AXES = ("x", "yl", "core", "zh", "zl", "yh")
BLK = ("x", "yl", "core")


def pack_kernel(k_ref, v_ref, id_ref, o_ref):
    ids = jnp.broadcast_to((id_ref[...] + 1).astype(jnp.float32), (16, ROWS)).astype(jnp.bfloat16)
    for g in range(Z):
        cols = slice(g * HEAD_DIM, (g + 1) * HEAD_DIM)
        o_ref[g, 0:ROWS, 0:HEAD_DIM] = k_ref[:, cols]
        o_ref[g, 0:ROWS, HEAD_DIM : 2 * HEAD_DIM] = v_ref[:, cols]
        o_ref[g, ROWS : ROWS + 16, 0:HEAD_DIM] = ids
        o_ref[g, ROWS : ROWS + 16, HEAD_DIM : 2 * HEAD_DIM] = ids


def attention_kernel(
    q_ref, own_ref, oth_ref, pown_ref, poth_ref, o_ref,
    k_buf, v_buf, ids_own, ids_oth, last_ref, lo_ref, s_ref, m_ref, acc_ref,
):
    odd = lax.axis_index("yh") == 1
    ones = jnp.ones((2 * ROWS, HEAD_DIM), jnp.bfloat16)
    for side, (a, b) in enumerate(((pown_ref, poth_ref), (own_ref, oth_ref))):
        for g in range(Z):
            p = side * Z + g
            for half, src in enumerate((a, b)):
                rows = slice(half * ROWS, (half + 1) * ROWS)
                k_buf[p, rows, :] = src[g, 0:ROWS, 0:HEAD_DIM]
                v_buf[p, rows, 0:HEAD_DIM] = src[g, 0:ROWS, HEAD_DIM : 2 * HEAD_DIM]
                ids = src[g, ROWS : ROWS + 16, 0:HEAD_DIM].astype(jnp.float32)[0:1, :]
                (ids_own if half == 0 else ids_oth)[p : p + 1, :] = ids
            v_buf[p, :, HEAD_DIM : 2 * HEAD_DIM] = ones
    last_ref[...] = jnp.broadcast_to(
        jnp.max(jnp.maximum(ids_own[...], ids_oth[...]), axis=1, keepdims=True), (PAIRS, ROWS)
    )
    for z in range(Z):
        first = jnp.min(ids_own[Z + z : Z + z + 1, :], axis=1, keepdims=True)
        before = jnp.where(last_ref[...] < first, 1.0 / ROWS, 0.0)
        lo_ref[z] = jnp.sum(before).astype(jnp.int32)

    def scores(q4, p):
        return lax.dot_general(
            q4, k_buf[p], (((1,), (1,)), ((), ())), preferred_element_type=jnp.float32
        )

    def weigh(slot, p):
        part = s_ref[slot]
        peak = jnp.concatenate([m_ref[...]] * 2, axis=1)
        weights = jnp.exp2((part - peak) * EXP2_SCALE).astype(jnp.bfloat16)
        return jnp.dot(weights, v_buf[p], preferred_element_type=jnp.float32)

    @pl.loop(0, Z)
    def _(z):
        q = q_ref[z]
        q4 = jnp.concatenate([q[:, g * HEAD_DIM : (g + 1) * HEAD_DIM] for g in range(GROUP)], axis=0)
        diag = Z + z
        count = jnp.clip(diag - lo_ref[z], 0, Z)
        steps = (count + 1) // 2
        qid = jnp.transpose(jnp.broadcast_to(ids_own[pl.ds(diag, 1), :], (ROWS, ROWS)))

        def put(slot, part, keep_own, keep_oth, start):
            for g in range(GROUP):
                rows = slice(g * ROWS, (g + 1) * ROWS)
                left = jnp.where(keep_own, part[rows, 0:ROWS], MASKED)
                right = jnp.where(keep_oth, part[rows, ROWS : 2 * ROWS], MASKED)
                s_ref[slot, rows, 0:ROWS] = left
                s_ref[slot, rows, ROWS : 2 * ROWS] = right
                most = jnp.maximum(left, right)
                m_ref[rows, :] = most if start else jnp.maximum(m_ref[rows, :], most)

        at_row = lax.broadcasted_iota(jnp.int32, (ROWS, ROWS), 0)
        at_col = lax.broadcasted_iota(jnp.int32, (ROWS, ROWS), 1)
        same_own = ids_own[pl.ds(diag, 1), :] == qid
        same_oth = ids_oth[pl.ds(diag, 1), :] == qid
        put(Z, scores(q4, diag), same_own & (at_col <= at_row), same_oth & odd, True)

        @pl.loop(0, steps)
        def _(k):
            for u in range(2):
                slot = 2 * k + u
                p = jnp.maximum(diag - 1 - slot, 0)
                put(
                    slot,
                    scores(q4, p),
                    ids_own[pl.ds(p, 1), :] == qid,
                    ids_oth[pl.ds(p, 1), :] == qid,
                    False,
                )

        m_ref[...] = jnp.broadcast_to(
            jnp.max(m_ref[...], axis=1, keepdims=True), (GROUP * ROWS, ROWS)
        )
        acc_ref[...] = weigh(Z, diag)

        @pl.loop(0, steps)
        def _(k):
            total = None
            for u in range(2):
                slot = 2 * k + u
                p = jnp.maximum(diag - 1 - slot, 0)
                term = weigh(slot, p)
                total = term if total is None else total + term
            acc_ref[...] += total

        zh, zl = z // 2, z % 2
        for g in range(GROUP):
            rows = slice(g * ROWS, (g + 1) * ROWS)
            out = acc_ref[rows, 0:HEAD_DIM] / acc_ref[rows, HEAD_DIM : 2 * HEAD_DIM]
            half = g // 2
            o_ref[
                2 * zh + g % 2, pl.ds(zl * ROWS, ROWS), half * HEAD_DIM : (half + 1) * HEAD_DIM
            ] = out.astype(jnp.bfloat16)


def projection_kernel(a_ref, w_ref, mine_ref, other_ref, a_buf):
    @pl.when(pl.program_id(0) == 0)
    def _():
        core = lax.axis_index("core")
        zl = lax.axis_index("zl")
        for zh in range(4):
            for t in range(2):
                source = 2 * zh + (core if t == 0 else 1 - core)
                for u in range(2):
                    row = (zl if u == 0 else 1 - zl) * ROWS
                    at = (2 * t + u) * ROWS
                    a_buf[at : at + ROWS, zh * 256 : (zh + 1) * 256] = a_ref[
                        source, pl.ds(row, ROWS), :
                    ]

    cols = w_ref.shape[-1]
    w = w_ref[0].reshape(8 * ROWS, cols)
    y = jnp.dot(a_buf[...], w, preferred_element_type=jnp.float32).astype(jnp.bfloat16)
    for u in range(2):
        mine_ref[u] = y[u * ROWS : (u + 1) * ROWS]
        other_ref[u] = y[(2 + u) * ROWS : (3 + u) * ROWS]


def body(queries, keys, values, doc_ids, out_weight):
    bf16 = jnp.bfloat16
    params = pltpu.CompilerParams(vmem_limit_bytes=VMEM_LIMIT)
    core = lax.axis_index("core")
    out_cols = out_weight.shape[1]
    piece = out_cols // 4

    own_part = lax.dynamic_slice(
        out_weight, (core * ROWS, lax.axis_index("x") * piece), (ROWS, piece)
    )
    weight = lax.all_gather(own_part, ("zh", "yh"), axis=0, tiled=False)
    weight = lax.all_gather(weight, "x", axis=0, tiled=False)

    packed = pl.pallas_call(
        pack_kernel,
        out_shape=jax.ShapeDtypeStruct((Z, ROWS + 16, 2 * HEAD_DIM), bf16),
        compiler_params=params,
        name="pack_kv",
    )(keys, values, doc_ids.reshape(1, ROWS))
    own = lax.all_to_all(packed, ("zh", "zl"), 0, 0, tiled=True)
    swap = [(0, 1), (1, 0)]
    ahead = [(i, i + 1) for i in range(15)]
    other = lax.ppermute(own, "yh", swap)
    prev_own = lax.ppermute(own, BLK, ahead)
    prev_other = lax.ppermute(other, BLK, ahead)

    split = queries.reshape(ROWS, Z, GROUP * HEAD_DIM).transpose(1, 0, 2)
    query = lax.all_to_all(split, ("zh", "zl"), 0, 0, tiled=True)

    attn = pl.pallas_call(
        attention_kernel,
        out_shape=jax.ShapeDtypeStruct((8, 2 * ROWS, 2 * HEAD_DIM), bf16),
        scratch_shapes=[
            pltpu.VMEM((PAIRS, 2 * ROWS, HEAD_DIM), bf16),
            pltpu.VMEM((PAIRS, 2 * ROWS, 2 * HEAD_DIM), bf16),
            pltpu.VMEM((PAIRS, ROWS), jnp.float32),
            pltpu.VMEM((PAIRS, ROWS), jnp.float32),
            pltpu.VMEM((PAIRS, ROWS), jnp.float32),
            pltpu.SMEM((Z,), jnp.int32),
            pltpu.VMEM((Z + 1, GROUP * ROWS, 2 * ROWS), jnp.float32),
            pltpu.VMEM((GROUP * ROWS, ROWS), jnp.float32),
            pltpu.VMEM((GROUP * ROWS, 2 * HEAD_DIM), jnp.float32),
        ],
        compiler_params=params,
        name="attention",
    )(query, own, other, prev_own, prev_other)

    spread = lax.all_to_all(attn, ("zh", "core"), 0, 0, tiled=True)
    half = jax.ShapeDtypeStruct((2, ROWS, out_cols), bf16)
    mine, theirs = pl.pallas_call(
        projection_kernel,
        grid=(4,),
        in_specs=[
            pl.BlockSpec((8, 2 * ROWS, 2 * HEAD_DIM), lambda i: (0, 0, 0)),
            pl.BlockSpec((1, 8, ROWS, piece), lambda i: (i, 0, 0, 0)),
        ],
        out_specs=[
            pl.BlockSpec((2, ROWS, piece), lambda i: (0, 0, i)),
            pl.BlockSpec((2, ROWS, piece), lambda i: (0, 0, i)),
        ],
        out_shape=[half, half],
        scratch_shapes=[pltpu.VMEM((4 * ROWS, 8 * ROWS), bf16)],
        compiler_params=params,
        name="projection",
    )(spread, weight)
    arrived = lax.ppermute(theirs, "core", swap)
    summed = mine.astype(jnp.float32) + arrived.astype(jnp.float32)
    last = lax.ppermute(summed[1].astype(bf16), "zl", swap)
    return (summed[0] + last.astype(jnp.float32)).astype(bf16)


def solution(mesh):
    torus = Mesh(mesh.devices.reshape(4, 2, 2, 4, 2, 2), AXES)
    uly = ("zh", "zl", "yh")
    rows = P(BLK + uly, None)
    in_specs = (rows, rows, rows, P(BLK + uly), P(uly, None))
    return jax.shard_map(body, mesh=torus, in_specs=in_specs, out_specs=rows, check_vma=False)
```

```python
import functools
import math

import jax
import jax.numpy as jnp
from jax import lax
from jax.experimental import pallas as pl
from jax.experimental.pallas import tpu as pltpu
from jax.sharding import Mesh
from jax.sharding import PartitionSpec as P

HEAD_DIM = 128
ROWS = 128
Z = 8
GROUP = 4
PAIRS = 16
EXP2_SCALE = math.log2(math.e) / math.sqrt(HEAD_DIM)
MASKED = -1e30
HALVES = 2
VMEM_LIMIT = 48 * 1024 * 1024

AXES = ("x", "yl", "core", "zh", "zl", "yh")
BLK = ("x", "yl", "core")


def pack_kernel(k_ref, v_ref, id_ref, o_ref):
    ids = jnp.broadcast_to((id_ref[...] + 1).astype(jnp.float32), (16, ROWS)).astype(jnp.bfloat16)
    for g in range(Z):
        cols = slice(g * HEAD_DIM, (g + 1) * HEAD_DIM)
        o_ref[g, 0:ROWS, 0:HEAD_DIM] = k_ref[:, cols]
        o_ref[g, 0:ROWS, HEAD_DIM : 2 * HEAD_DIM] = v_ref[:, cols]
        o_ref[g, ROWS : ROWS + 16, 0:HEAD_DIM] = ids
        o_ref[g, ROWS : ROWS + 16, HEAD_DIM : 2 * HEAD_DIM] = ids


def attention_kernel(
    q_ref, own_ref, oth_ref, pown_ref, poth0_ref, poth1_ref, o_ref,
    k_buf, v_buf, ids_own, ids_oth, last_ref, lo_ref, s_ref, m_ref, acc_ref,
):
    odd = lax.axis_index("yh") == 1
    ones = jnp.ones((2 * ROWS, HEAD_DIM), jnp.bfloat16)
    for side, (a, b) in enumerate((((pown_ref,), (poth0_ref, poth1_ref)), ((own_ref,), (oth_ref,)))):
        for g in range(Z):
            p = side * Z + g
            for half, parts in enumerate((a, b)):
                block = parts[0][g] if len(parts) == 1 else parts[0][g] + parts[1][g]
                rows = slice(half * ROWS, (half + 1) * ROWS)
                k_buf[p, rows, :] = block[0:ROWS, 0:HEAD_DIM]
                v_buf[p, rows, 0:HEAD_DIM] = block[0:ROWS, HEAD_DIM : 2 * HEAD_DIM]
                ids = block[ROWS : ROWS + 16, 0:HEAD_DIM].astype(jnp.float32)[0:1, :]
                (ids_own if half == 0 else ids_oth)[p : p + 1, :] = ids
            v_buf[p, :, HEAD_DIM : 2 * HEAD_DIM] = ones
    last_ref[...] = jnp.broadcast_to(
        jnp.max(jnp.maximum(ids_own[...], ids_oth[...]), axis=1, keepdims=True), (PAIRS, ROWS)
    )
    for z in range(Z):
        first = jnp.min(ids_own[Z + z : Z + z + 1, :], axis=1, keepdims=True)
        before = jnp.where(last_ref[...] < first, 1.0 / ROWS, 0.0)
        lo_ref[z] = jnp.sum(before).astype(jnp.int32)

    def scores(q4, p):
        return lax.dot_general(
            q4, k_buf[p], (((1,), (1,)), ((), ())), preferred_element_type=jnp.float32
        )

    def weigh(slot, p):
        part = s_ref[slot]
        peak = jnp.concatenate([m_ref[...]] * 2, axis=1)
        weights = jnp.exp2((part - peak) * EXP2_SCALE).astype(jnp.bfloat16)
        return jnp.dot(weights, v_buf[p], preferred_element_type=jnp.float32)

    @pl.loop(0, Z)
    def _(z):
        q = q_ref[z]
        q4 = jnp.concatenate([q[:, g * HEAD_DIM : (g + 1) * HEAD_DIM] for g in range(GROUP)], axis=0)
        diag = Z + z
        count = jnp.clip(diag - lo_ref[z], 0, Z)
        steps = (count + 1) // 2
        qid = jnp.transpose(jnp.broadcast_to(ids_own[pl.ds(diag, 1), :], (ROWS, ROWS)))

        def put(slot, part, keep_own, keep_oth, start):
            for g in range(GROUP):
                rows = slice(g * ROWS, (g + 1) * ROWS)
                left = jnp.where(keep_own, part[rows, 0:ROWS], MASKED)
                right = jnp.where(keep_oth, part[rows, ROWS : 2 * ROWS], MASKED)
                s_ref[slot, rows, 0:ROWS] = left
                s_ref[slot, rows, ROWS : 2 * ROWS] = right
                most = jnp.maximum(left, right)
                m_ref[rows, :] = most if start else jnp.maximum(m_ref[rows, :], most)

        at_row = lax.broadcasted_iota(jnp.int32, (ROWS, ROWS), 0)
        at_col = lax.broadcasted_iota(jnp.int32, (ROWS, ROWS), 1)
        same_own = ids_own[pl.ds(diag, 1), :] == qid
        same_oth = ids_oth[pl.ds(diag, 1), :] == qid
        put(Z, scores(q4, diag), same_own & (at_col <= at_row), same_oth & odd, True)

        @pl.loop(0, steps)
        def _(k):
            for u in range(2):
                slot = 2 * k + u
                p = jnp.maximum(diag - 1 - slot, 0)
                put(
                    slot,
                    scores(q4, p),
                    ids_own[pl.ds(p, 1), :] == qid,
                    ids_oth[pl.ds(p, 1), :] == qid,
                    False,
                )

        m_ref[...] = jnp.broadcast_to(
            jnp.max(m_ref[...], axis=1, keepdims=True), (GROUP * ROWS, ROWS)
        )
        acc_ref[...] = weigh(Z, diag)

        @pl.loop(0, steps)
        def _(k):
            total = None
            for u in range(2):
                slot = 2 * k + u
                p = jnp.maximum(diag - 1 - slot, 0)
                term = weigh(slot, p)
                total = term if total is None else total + term
            acc_ref[...] += total

        for g in range(GROUP):
            rows = slice(g * ROWS, (g + 1) * ROWS)
            out = acc_ref[rows, 0:HEAD_DIM] / acc_ref[rows, HEAD_DIM : 2 * HEAD_DIM]
            o_ref[4 * z + 2 * (g % 2) + g // 2] = out.astype(jnp.bfloat16)


def projection_kernel(a_ref, w_ref, mine_ref, other_ref, a_buf):
    @pl.when(pl.program_id(0) == 0)
    def _():
        core = lax.axis_index("core")
        yl = lax.axis_index("yl")
        for t in range(2):
            for u in range(2):
                source = 2 * (core if t == 0 else 1 - core) + (yl if u == 0 else 1 - yl)
                at = (2 * t + u) * ROWS
                for z in range(Z):
                    a_buf[at : at + ROWS, z * ROWS : (z + 1) * ROWS] = a_ref[4 * z + source]

    w = w_ref[0].reshape(Z * ROWS, w_ref.shape[-1])
    y = jnp.dot(a_buf[...], w, preferred_element_type=jnp.float32).astype(jnp.bfloat16)
    for u in range(2):
        mine_ref[u] = y[u * ROWS : (u + 1) * ROWS]
        other_ref[u] = y[(2 + u) * ROWS : (3 + u) * ROWS]


def body(queries, keys, values, doc_ids, out_weight):
    bf16 = jnp.bfloat16
    params = pltpu.CompilerParams(vmem_limit_bytes=VMEM_LIMIT)
    core = lax.axis_index("core")
    out_cols = out_weight.shape[1]
    cols = out_cols // HALVES
    piece = cols // 4
    swap = [(0, 1), (1, 0)]

    packed = pl.pallas_call(
        pack_kernel,
        out_shape=jax.ShapeDtypeStruct((Z, ROWS + 16, 2 * HEAD_DIM), bf16),
        compiler_params=params,
        name="pack_kv",
    )(keys, values, doc_ids.reshape(1, ROWS))
    mine = [
        lax.dynamic_slice(
            out_weight, (core * ROWS, j * cols + lax.axis_index("x") * piece), (ROWS, piece)
        )
        for j in range(HALVES)
    ]
    mine, packed = lax.optimization_barrier((jnp.stack(mine), packed))
    mine = lax.ppermute(mine, ("yl", "yh"), [(0, 0), (1, 2), (2, 1), (3, 3)])
    weights = [lax.all_gather(mine[j], ("x", "zh", "zl"), axis=0, tiled=False) for j in range(HALVES)]

    own = lax.all_to_all(packed, ("zh", "zl"), 0, 0, tiled=True)
    other = lax.ppermute(own, "yh", swap)
    prev_own = lax.ppermute(own, BLK, [(i, i + 1) for i in range(15)])
    prev_other_0 = lax.ppermute(
        own,
        BLK + ("yh",),
        [(2 * i + h, 2 * (i + 1) + 1 - h) for i in range(1, 15, 2) for h in range(2)],
    )
    prev_other_1 = lax.ppermute(other, "core", [(0, 1)])

    split = queries.reshape(ROWS, Z, GROUP * HEAD_DIM).transpose(1, 0, 2)
    query = lax.all_to_all(split, ("zh", "zl"), 0, 0, tiled=True)

    attn = pl.pallas_call(
        attention_kernel,
        out_shape=jax.ShapeDtypeStruct((4 * Z, ROWS, HEAD_DIM), bf16),
        scratch_shapes=[
            pltpu.VMEM((PAIRS, 2 * ROWS, HEAD_DIM), bf16),
            pltpu.VMEM((PAIRS, 2 * ROWS, 2 * HEAD_DIM), bf16),
            pltpu.VMEM((PAIRS, ROWS), jnp.float32),
            pltpu.VMEM((PAIRS, ROWS), jnp.float32),
            pltpu.VMEM((PAIRS, ROWS), jnp.float32),
            pltpu.SMEM((Z,), jnp.int32),
            pltpu.VMEM((Z + 1, GROUP * ROWS, 2 * ROWS), jnp.float32),
            pltpu.VMEM((GROUP * ROWS, ROWS), jnp.float32),
            pltpu.VMEM((GROUP * ROWS, 2 * HEAD_DIM), jnp.float32),
        ],
        compiler_params=params,
        cost_estimate=pl.CostEstimate(
            flops=2_000_000_000, bytes_accessed=6_000_000, transcendentals=4_000_000
        ),
        name="attention",
    )(query, own, other, prev_own, prev_other_0, prev_other_1)

    spread = lax.all_to_all(attn, ("zh", "zl", "core", "yl"), 0, 0, tiled=True)
    half = jax.ShapeDtypeStruct((2, ROWS, cols), bf16)

    def finish(summed):
        last = lax.ppermute(summed[1].astype(bf16), "yl", swap)
        return (summed[0] + last.astype(jnp.float32)).astype(bf16)

    parts = []
    for j in range(HALVES):
        if parts:
            spread, summed = lax.optimization_barrier((spread, summed))
            parts[-1] = finish(summed)
        own_sum, theirs = pl.pallas_call(
            projection_kernel,
            grid=(4,),
            in_specs=[
                pl.BlockSpec((4 * Z, ROWS, HEAD_DIM), lambda i: (0, 0, 0)),
                pl.BlockSpec((1, Z, ROWS, piece), lambda i: (i, 0, 0, 0)),
            ],
            out_specs=[
                pl.BlockSpec((2, ROWS, piece), lambda i: (0, 0, i)),
                pl.BlockSpec((2, ROWS, piece), lambda i: (0, 0, i)),
            ],
            out_shape=[half, half],
            scratch_shapes=[pltpu.VMEM((4 * ROWS, Z * ROWS), bf16)],
            compiler_params=params,
            cost_estimate=pl.CostEstimate(
                flops=2 * 4 * ROWS * Z * ROWS * cols,
                bytes_accessed=2 * Z * ROWS * cols + 8 * ROWS * cols,
                transcendentals=0,
            ),
            name="projection",
        )(spread, weights[j].reshape(4, Z, ROWS, piece))
        arrived = lax.ppermute(theirs, "core", swap)
        summed = own_sum.astype(jnp.float32) + arrived.astype(jnp.float32)
        parts.append(None)
    parts[-1] = finish(summed)
    return jnp.concatenate(parts, axis=1)


def solution(mesh):
    torus = Mesh(mesh.devices.reshape(4, 2, 2, 4, 2, 2), AXES)
    uly = ("zh", "zl", "yh")
    rows = P(BLK + uly, None)
    in_specs = (rows, rows, rows, P(BLK + uly), P(uly, None))
    return jax.shard_map(body, mesh=torus, in_specs=in_specs, out_specs=rows, check_vma=False)
```

```python
import functools
import math

import jax
import jax.numpy as jnp
from jax import lax
from jax.experimental import pallas as pl
from jax.experimental.pallas import tpu as pltpu
from jax.sharding import Mesh
from jax.sharding import PartitionSpec as P

HEAD_DIM = 128
ROWS = 128
Z = 8
GROUP = 4
PAIRS = 16
EXP2_SCALE = math.log2(math.e) / math.sqrt(HEAD_DIM)
MASKED = -1e30
HALVES = 2
VMEM_LIMIT = 20 * 1024 * 1024

AXES = ("x", "yl", "core", "zh", "zl", "yh")
BLK = ("x", "yl", "core")


def pack_kernel(k_ref, v_ref, id_ref, o_ref):
    ids = jnp.broadcast_to((id_ref[...] + 1).astype(jnp.float32), (16, ROWS)).astype(jnp.bfloat16)
    for g in range(Z):
        cols = slice(g * HEAD_DIM, (g + 1) * HEAD_DIM)
        o_ref[g, 0:ROWS, 0:HEAD_DIM] = k_ref[:, cols]
        o_ref[g, 0:ROWS, HEAD_DIM : 2 * HEAD_DIM] = v_ref[:, cols]
        o_ref[g, ROWS : ROWS + 16, 0:HEAD_DIM] = ids
        o_ref[g, ROWS : ROWS + 16, HEAD_DIM : 2 * HEAD_DIM] = ids


def attention_kernel(
    q_ref, own_ref, oth_ref, pown_ref, poth0_ref, poth1_ref, o_ref,
    k_buf, v_buf, ids_own, ids_oth, last_ref, lo_ref, s_ref, m_ref, acc_ref,
):
    odd = lax.axis_index("yh") == 1
    ones = jnp.ones((2 * ROWS, HEAD_DIM), jnp.bfloat16)
    for side, (a, b) in enumerate((((pown_ref,), (poth0_ref, poth1_ref)), ((own_ref,), (oth_ref,)))):
        for g in range(Z):
            p = side * Z + g
            for half, parts in enumerate((a, b)):
                block = parts[0][g] if len(parts) == 1 else parts[0][g] + parts[1][g]
                rows = slice(half * ROWS, (half + 1) * ROWS)
                k_buf[p, rows, :] = block[0:ROWS, 0:HEAD_DIM]
                v_buf[p, rows, 0:HEAD_DIM] = block[0:ROWS, HEAD_DIM : 2 * HEAD_DIM]
                ids = block[ROWS : ROWS + 16, 0:HEAD_DIM].astype(jnp.float32)[0:1, :]
                (ids_own if half == 0 else ids_oth)[p : p + 1, :] = ids
            v_buf[p, :, HEAD_DIM : 2 * HEAD_DIM] = ones
    last_ref[...] = jnp.broadcast_to(
        jnp.max(jnp.maximum(ids_own[...], ids_oth[...]), axis=1, keepdims=True), (PAIRS, ROWS)
    )
    for z in range(Z):
        first = jnp.min(ids_own[Z + z : Z + z + 1, :], axis=1, keepdims=True)
        before = jnp.where(last_ref[...] < first, 1.0 / ROWS, 0.0)
        lo_ref[z] = jnp.sum(before).astype(jnp.int32)

    def scores(q4, p):
        return lax.dot_general(
            q4, k_buf[p], (((1,), (1,)), ((), ())), preferred_element_type=jnp.float32
        )

    def weigh(slot, p):
        part = s_ref[slot]
        peak = jnp.concatenate([m_ref[...]] * 2, axis=1)
        weights = jnp.exp2((part - peak) * EXP2_SCALE).astype(jnp.bfloat16)
        return jnp.dot(weights, v_buf[p], preferred_element_type=jnp.float32)

    @pl.loop(0, Z)
    def _(z):
        q = q_ref[z]
        q4 = jnp.concatenate([q[:, g * HEAD_DIM : (g + 1) * HEAD_DIM] for g in range(GROUP)], axis=0)
        diag = Z + z
        count = jnp.clip(diag - lo_ref[z], 0, Z)
        steps = (count + 1) // 2
        qid = jnp.transpose(jnp.broadcast_to(ids_own[pl.ds(diag, 1), :], (ROWS, ROWS)))

        def put(slot, part, keep_own, keep_oth, start):
            for g in range(GROUP):
                rows = slice(g * ROWS, (g + 1) * ROWS)
                left = jnp.where(keep_own, part[rows, 0:ROWS], MASKED)
                right = jnp.where(keep_oth, part[rows, ROWS : 2 * ROWS], MASKED)
                s_ref[slot, rows, 0:ROWS] = left
                s_ref[slot, rows, ROWS : 2 * ROWS] = right
                most = jnp.maximum(left, right)
                m_ref[rows, :] = most if start else jnp.maximum(m_ref[rows, :], most)

        at_row = lax.broadcasted_iota(jnp.int32, (ROWS, ROWS), 0)
        at_col = lax.broadcasted_iota(jnp.int32, (ROWS, ROWS), 1)
        same_own = ids_own[pl.ds(diag, 1), :] == qid
        same_oth = ids_oth[pl.ds(diag, 1), :] == qid
        put(Z, scores(q4, diag), same_own & (at_col <= at_row), same_oth & odd, True)

        @pl.loop(0, steps)
        def _(k):
            for u in range(2):
                slot = 2 * k + u
                p = jnp.maximum(diag - 1 - slot, 0)
                put(
                    slot,
                    scores(q4, p),
                    ids_own[pl.ds(p, 1), :] == qid,
                    ids_oth[pl.ds(p, 1), :] == qid,
                    False,
                )

        m_ref[...] = jnp.broadcast_to(
            jnp.max(m_ref[...], axis=1, keepdims=True), (GROUP * ROWS, ROWS)
        )
        acc_ref[...] = weigh(Z, diag)

        @pl.loop(0, steps)
        def _(k):
            total = None
            for u in range(2):
                slot = 2 * k + u
                p = jnp.maximum(diag - 1 - slot, 0)
                term = weigh(slot, p)
                total = term if total is None else total + term
            acc_ref[...] += total

        for g in range(GROUP):
            rows = slice(g * ROWS, (g + 1) * ROWS)
            out = acc_ref[rows, 0:HEAD_DIM] / acc_ref[rows, HEAD_DIM : 2 * HEAD_DIM]
            o_ref[4 * z + 2 * (g % 2) + g // 2] = out.astype(jnp.bfloat16)


def projection_kernel(a_ref, own_ref, before_ref, after_ref, far0_ref, far1_ref, keep_ref, send_ref, other_ref, a_buf):
    core = lax.axis_index("core")
    yl = lax.axis_index("yl")
    x = lax.axis_index("x")
    for t in range(2):
        for u in range(2):
            source = 2 * (core if t == 0 else 1 - core) + (yl if u == 0 else 1 - yl)
            at = (2 * t + u) * ROWS
            for z in range(Z):
                a_buf[at : at + ROWS, z * ROWS : (z + 1) * ROWS] = a_ref[4 * z + source]
    piece = own_ref.shape[-1]
    half = (Z // 2) * ROWS

    def product(rows, part):
        return jnp.dot(a_buf[:, rows], part, preferred_element_type=jnp.float32)

    for shift in (0, 3, 1, 2):
        if shift == 2:
            y = product(slice(0, half), far0_ref[...].reshape(half, piece))
            y = y + product(slice(half, 2 * half), far1_ref[...].reshape(half, piece))
        else:
            ref = {0: own_ref, 3: before_ref, 1: after_ref}[shift]
            y = product(slice(0, 2 * half), ref[...].reshape(2 * half, piece))
        y = y.astype(jnp.bfloat16)
        cols = pl.ds(pl.multiple_of(lax.rem(x + shift, 4) * piece, piece), piece)
        keep_ref[:, cols] = y[0:ROWS]
        send_ref[:, cols] = y[ROWS : 2 * ROWS]
        for u in range(2):
            other_ref[u, :, cols] = y[(2 + u) * ROWS : (3 + u) * ROWS]


def body(queries, keys, values, doc_ids, out_weight):
    bf16 = jnp.bfloat16
    params = pltpu.CompilerParams(vmem_limit_bytes=VMEM_LIMIT)
    core = lax.axis_index("core")
    out_cols = out_weight.shape[1]
    cols = out_cols // HALVES
    piece = cols // 4
    swap = [(0, 1), (1, 0)]

    packed = pl.pallas_call(
        pack_kernel,
        out_shape=jax.ShapeDtypeStruct((Z, ROWS + 16, 2 * HEAD_DIM), bf16),
        compiler_params=params,
        name="pack_kv",
    )(keys, values, doc_ids.reshape(1, ROWS))
    mine = [
        lax.dynamic_slice(
            out_weight, (core * ROWS, j * cols + lax.axis_index("x") * piece), (ROWS, piece)
        )
        for j in range(HALVES)
    ]
    mine, packed = lax.optimization_barrier((jnp.stack(mine), packed))
    mine = lax.ppermute(mine, ("yl", "yh"), [(0, 0), (1, 2), (2, 1), (3, 3)])
    right = [(i, (i + 1) % 4) for i in range(4)]
    left = [((i + 1) % 4, i) for i in range(4)]
    here = [lax.all_gather(mine[j], ("zh", "zl"), axis=0, tiled=False) for j in range(HALVES)]

    def beside(j):
        return lax.ppermute(here[j], "x", right), lax.ppermute(here[j], "x", left)

    def beyond(before, after):
        return (
            lax.ppermute(before[: Z // 2], "x", right),
            lax.ppermute(after[Z // 2 :], "x", left),
        )

    own = lax.all_to_all(packed, ("zh", "zl"), 0, 0, tiled=True)
    own, here[0] = lax.optimization_barrier((own, here[0]))
    near0 = beside(0)
    other = lax.ppermute(own, "yh", swap)
    prev_own = lax.ppermute(own, BLK, [(i, i + 1) for i in range(15)])
    prev_other_0 = lax.ppermute(
        own,
        BLK + ("yh",),
        [(2 * i + h, 2 * (i + 1) + 1 - h) for i in range(1, 15, 2) for h in range(2)],
    )
    prev_other_1 = lax.ppermute(other, "core", [(0, 1)])

    split = queries.reshape(ROWS, Z, GROUP * HEAD_DIM).transpose(1, 0, 2)
    query = lax.all_to_all(split, ("zh", "zl"), 0, 0, tiled=True)

    query, near0, here[1] = lax.optimization_barrier((query, near0, here[1]))
    far0 = beyond(*near0)
    near1 = beside(1)
    attn = pl.pallas_call(
        attention_kernel,
        out_shape=jax.ShapeDtypeStruct((4 * Z, ROWS, HEAD_DIM), bf16),
        scratch_shapes=[
            pltpu.VMEM((PAIRS, 2 * ROWS, HEAD_DIM), bf16),
            pltpu.VMEM((PAIRS, 2 * ROWS, 2 * HEAD_DIM), bf16),
            pltpu.VMEM((PAIRS, ROWS), jnp.float32),
            pltpu.VMEM((PAIRS, ROWS), jnp.float32),
            pltpu.VMEM((PAIRS, ROWS), jnp.float32),
            pltpu.SMEM((Z,), jnp.int32),
            pltpu.VMEM((Z + 1, GROUP * ROWS, 2 * ROWS), jnp.float32),
            pltpu.VMEM((GROUP * ROWS, ROWS), jnp.float32),
            pltpu.VMEM((GROUP * ROWS, 2 * HEAD_DIM), jnp.float32),
        ],
        compiler_params=params,
        cost_estimate=pl.CostEstimate(
            flops=16_000_000_000, bytes_accessed=6_000_000, transcendentals=4_000_000
        ),
        name="attention",
    )(query, own, other, prev_own, prev_other_0, prev_other_1)

    attn, far0 = lax.optimization_barrier((attn, far0))
    spread = lax.all_to_all(attn, ("zh", "zl", "core", "yl"), 0, 0, tiled=True)
    spread, near1 = lax.optimization_barrier((spread, near1))
    far1 = beyond(*near1)
    weights = ((here[0], *near0, *far0), (here[1], *near1, *far1))
    one = jax.ShapeDtypeStruct((ROWS, cols), bf16)
    two = jax.ShapeDtypeStruct((2, ROWS, cols), bf16)
    f32 = jnp.float32
    parts = []
    for j in range(HALVES):
        keep, send, theirs = pl.pallas_call(
            projection_kernel,
            out_shape=[one, one, two],
            scratch_shapes=[pltpu.VMEM((4 * ROWS, Z * ROWS), bf16)],
            compiler_params=params,
            cost_estimate=pl.CostEstimate(
                flops=2 * 4 * ROWS * Z * ROWS * cols,
                bytes_accessed=2 * Z * ROWS * cols + 8 * ROWS * cols,
                transcendentals=0,
            ),
            name="projection",
        )(spread, *weights[j])
        arrived = lax.ppermute(theirs, "core", swap)
        send = (send.astype(f32) + arrived[1].astype(f32)).astype(bf16)
        if j + 1 < HALVES:
            spread, send = lax.optimization_barrier((spread, send))
        parts.append((keep, arrived[0], lax.ppermute(send, "yl", swap)))
    return jnp.concatenate(
        [(k.astype(f32) + a.astype(f32) + m.astype(f32)).astype(bf16) for k, a, m in parts], axis=1
    )


def solution(mesh):
    torus = Mesh(mesh.devices.reshape(4, 2, 2, 4, 2, 2), AXES)
    uly = ("zh", "zl", "yh")
    rows = P(BLK + uly, None)
    in_specs = (rows, rows, rows, P(BLK + uly), P(uly, None))
    return jax.shard_map(body, mesh=torus, in_specs=in_specs, out_specs=rows, check_vma=False)
```

```python
import functools
import math

import jax
import jax.numpy as jnp
from jax import lax
from jax.experimental import pallas as pl
from jax.experimental.pallas import tpu as pltpu
from jax.sharding import Mesh
from jax.sharding import PartitionSpec as P

HEAD_DIM = 128
ROWS = 128
Z = 8
GROUP = 4
PAIRS = 16
EXP2_SCALE = math.log2(math.e) / math.sqrt(HEAD_DIM)
MASKED = -1e30
Z_ORDER = (0, 7, 1, 6, 2, 5, 3, 4)
HALVES = 2
VMEM_LIMIT = 56 * 1024 * 1024

AXES = ("x", "yl", "core", "zh", "zl", "yh")
BLK = ("x", "yl", "core")


def pack_kernel(k_ref, v_ref, id_ref, o_ref):
    ids = jnp.broadcast_to((id_ref[...] + 1).astype(jnp.float32), (16, ROWS)).astype(jnp.bfloat16)
    for g in range(Z):
        cols = slice(g * HEAD_DIM, (g + 1) * HEAD_DIM)
        o_ref[g, 0:ROWS, 0:HEAD_DIM] = k_ref[:, cols]
        o_ref[g, 0:ROWS, HEAD_DIM : 2 * HEAD_DIM] = v_ref[:, cols]
        o_ref[g, ROWS : ROWS + 16, 0:HEAD_DIM] = ids
        o_ref[g, ROWS : ROWS + 16, HEAD_DIM : 2 * HEAD_DIM] = ids


def attention_kernel(
    q_ref, own_ref, oth_ref, pown_ref, poth0_ref, poth1_ref, o_ref,
    k_buf, v_buf, ids_own, ids_oth, last_ref, lo_ref, s_ref, m_ref, acc_ref,
):
    odd = lax.axis_index("yh") == 1
    ones = jnp.ones((2 * ROWS, HEAD_DIM), jnp.bfloat16)
    for side, (a, b) in enumerate((((pown_ref,), (poth0_ref, poth1_ref)), ((own_ref,), (oth_ref,)))):
        for g in range(Z):
            p = side * Z + g
            for half, parts in enumerate((a, b)):
                block = parts[0][g] if len(parts) == 1 else parts[0][g] + parts[1][g]
                rows = slice(half * ROWS, (half + 1) * ROWS)
                k_buf[p, rows, :] = block[0:ROWS, 0:HEAD_DIM]
                v_buf[p, rows, 0:HEAD_DIM] = block[0:ROWS, HEAD_DIM : 2 * HEAD_DIM]
                ids = block[ROWS : ROWS + 16, 0:HEAD_DIM].astype(jnp.float32)[0:1, :]
                (ids_own if half == 0 else ids_oth)[p : p + 1, :] = ids
            v_buf[p, :, HEAD_DIM : 2 * HEAD_DIM] = ones
    last_ref[...] = jnp.broadcast_to(
        jnp.max(jnp.maximum(ids_own[...], ids_oth[...]), axis=1, keepdims=True), (PAIRS, ROWS)
    )
    for z in range(Z):
        first = jnp.min(ids_own[Z + z : Z + z + 1, :], axis=1, keepdims=True)
        before = jnp.where(last_ref[...] < first, 1.0 / ROWS, 0.0)
        lo_ref[z] = jnp.sum(before).astype(jnp.int32)

    def scores(q4, p):
        return lax.dot_general(
            q4, k_buf[p], (((1,), (1,)), ((), ())), preferred_element_type=jnp.float32
        )

    def weigh(slot, p):
        part = s_ref[slot]
        peak = jnp.concatenate([m_ref[...]] * 2, axis=1)
        weights = jnp.exp2((part - peak) * EXP2_SCALE).astype(jnp.bfloat16)
        return jnp.dot(weights, v_buf[p], preferred_element_type=jnp.float32)

    @pl.loop(0, Z)
    def _(z):
        q = q_ref[z]
        q4 = jnp.concatenate([q[:, g * HEAD_DIM : (g + 1) * HEAD_DIM] for g in range(GROUP)], axis=0)
        diag = Z + z
        count = jnp.clip(diag - lo_ref[z], 0, Z)
        steps = (count + 1) // 2
        qid = jnp.transpose(jnp.broadcast_to(ids_own[pl.ds(diag, 1), :], (ROWS, ROWS)))

        def put(slot, part, keep_own, keep_oth, start):
            for g in range(GROUP):
                rows = slice(g * ROWS, (g + 1) * ROWS)
                left = jnp.where(keep_own, part[rows, 0:ROWS], MASKED)
                right = jnp.where(keep_oth, part[rows, ROWS : 2 * ROWS], MASKED)
                s_ref[slot, rows, 0:ROWS] = left
                s_ref[slot, rows, ROWS : 2 * ROWS] = right
                most = jnp.maximum(left, right)
                m_ref[rows, :] = most if start else jnp.maximum(m_ref[rows, :], most)

        at_row = lax.broadcasted_iota(jnp.int32, (ROWS, ROWS), 0)
        at_col = lax.broadcasted_iota(jnp.int32, (ROWS, ROWS), 1)
        same_own = ids_own[pl.ds(diag, 1), :] == qid
        same_oth = ids_oth[pl.ds(diag, 1), :] == qid
        put(Z, scores(q4, diag), same_own & (at_col <= at_row), same_oth & odd, True)

        @pl.loop(0, steps)
        def _(k):
            for u in range(2):
                slot = 2 * k + u
                p = jnp.maximum(diag - 1 - slot, 0)
                put(
                    slot,
                    scores(q4, p),
                    ids_own[pl.ds(p, 1), :] == qid,
                    ids_oth[pl.ds(p, 1), :] == qid,
                    False,
                )

        m_ref[...] = jnp.broadcast_to(
            jnp.max(m_ref[...], axis=1, keepdims=True), (GROUP * ROWS, ROWS)
        )
        acc_ref[...] = weigh(Z, diag)

        @pl.loop(0, steps)
        def _(k):
            total = None
            for u in range(2):
                slot = 2 * k + u
                p = jnp.maximum(diag - 1 - slot, 0)
                term = weigh(slot, p)
                total = term if total is None else total + term
            acc_ref[...] += total

        for g in range(GROUP):
            rows = slice(g * ROWS, (g + 1) * ROWS)
            out = acc_ref[rows, 0:HEAD_DIM] / acc_ref[rows, HEAD_DIM : 2 * HEAD_DIM]
            o_ref[4 * z + 2 * (g % 2) + g // 2] = out.astype(jnp.bfloat16)


def projection_kernel(a_ref, *refs):
    w_refs, (keep_ref, send_ref, other_ref, a_buf) = refs[:-4], refs[-4:]
    core = lax.axis_index("core")
    yl = lax.axis_index("yl")
    z_here = 2 * lax.axis_index("zh") + lax.axis_index("zl")
    x = lax.axis_index("x")
    for t in range(2):
        for u in range(2):
            source = 2 * (core if t == 0 else 1 - core) + (yl if u == 0 else 1 - yl)
            at = (2 * t + u) * ROWS
            for k, shift in enumerate(Z_ORDER):
                z = lax.rem(z_here + shift, Z)
                a_buf[at : at + ROWS, k * ROWS : (k + 1) * ROWS] = a_ref[4 * z + source]
    piece = keep_ref.shape[-1] // 4
    for n, shift in enumerate((0, 3, 1, 2)):
        y, at = None, 0
        for ref in w_refs[3 * n : 3 * n + 3]:
            depth = ref.shape[0] * ROWS
            part = ref[...].reshape(depth, piece)
            term = jnp.dot(a_buf[:, at : at + depth], part, preferred_element_type=jnp.float32)
            y, at = (term if y is None else y + term), at + depth
        y = y.astype(jnp.bfloat16)
        cols = pl.ds(pl.multiple_of(lax.rem(x + shift, 4) * piece, piece), piece)
        keep_ref[:, cols] = y[0:ROWS]
        send_ref[:, cols] = y[ROWS : 2 * ROWS]
        for u in range(2):
            other_ref[u, :, cols] = y[(2 + u) * ROWS : (3 + u) * ROWS]


def column_half(j, _):
    return 0, 0, j


def finish_kernel(*refs):
    o_ref, piece = refs[-1], refs[0].shape[-1] // 4
    for j in range(HALVES):
        keep, arrived, last = refs[3 * j : 3 * j + 3]
        for n in range(4):
            cols = slice(n * piece, (n + 1) * piece)
            total = keep[:, cols].astype(jnp.float32) + arrived[0, :, cols].astype(jnp.float32)
            total = total + last[:, cols].astype(jnp.float32)
            at = (HALVES * n + j) * piece
            o_ref[:, at : at + piece] = total.astype(jnp.bfloat16)


def body(queries, keys, values, doc_ids, out_weight):
    bf16 = jnp.bfloat16
    params = pltpu.CompilerParams(vmem_limit_bytes=VMEM_LIMIT)
    core = lax.axis_index("core")
    out_cols = out_weight.shape[1]
    cols = out_cols // HALVES
    swap = [(0, 1), (1, 0)]

    packed = pl.pallas_call(
        pack_kernel,
        out_shape=jax.ShapeDtypeStruct((Z, ROWS + 16, 2 * HEAD_DIM), bf16),
        compiler_params=params,
        name="pack_kv",
    )(keys, values, doc_ids.reshape(1, ROWS))
    def ring(axis, size, step):
        return lambda a: lax.ppermute(a, axis, [(i, (i + step) % size) for i in range(size)])

    z_up, z_down = ring(("zh", "zl"), Z, 1), ring(("zh", "zl"), Z, -1)
    x_up, x_down = ring("x", 4, 1), ring("x", 4, -1)

    def beside(group):
        return x_up(group), x_down(group)

    piece = lax.dynamic_slice(
        out_weight, (core * ROWS, lax.axis_index("x") * (out_cols // 4)), (ROWS, out_cols // 4)
    )
    piece = lax.ppermute(piece, ("yl", "yh"), [(0, 0), (1, 2), (2, 1), (3, 3)])
    up1, down1 = z_up(piece), z_down(piece)

    own = lax.all_to_all(packed, ("zh", "zl"), 0, 0, tiled=True)
    own, up1, down1 = lax.optimization_barrier((own, up1, down1))
    group1 = jnp.stack([piece, up1, down1])
    near1 = beside(group1)
    up2, down2 = z_up(up1), z_down(down1)
    up3, down3 = z_up(up2), z_down(down2)
    group2 = jnp.stack([up2, down2, up3, down3])
    group3 = z_up(up3)[None]
    other = lax.ppermute(own, "yh", swap)
    prev_own = lax.ppermute(own, BLK, [(i, i + 1) for i in range(15)])
    prev_other_0 = lax.ppermute(
        own,
        BLK + ("yh",),
        [(2 * i + h, 2 * (i + 1) + 1 - h) for i in range(1, 15, 2) for h in range(2)],
    )
    prev_other_1 = lax.ppermute(other, "core", [(0, 1)])

    split = queries.reshape(ROWS, Z, GROUP * HEAD_DIM).transpose(1, 0, 2)
    query = lax.all_to_all(split, ("zh", "zl"), 0, 0, tiled=True)

    query, near1, group2, group3 = lax.optimization_barrier((query, near1, group2, group3))
    far1 = x_up(near1[0])
    near2, near3 = beside(group2), beside(group3)
    attn = pl.pallas_call(
        attention_kernel,
        out_shape=jax.ShapeDtypeStruct((4 * Z, ROWS, HEAD_DIM), bf16),
        scratch_shapes=[
            pltpu.VMEM((PAIRS, 2 * ROWS, HEAD_DIM), bf16),
            pltpu.VMEM((PAIRS, 2 * ROWS, 2 * HEAD_DIM), bf16),
            pltpu.VMEM((PAIRS, ROWS), jnp.float32),
            pltpu.VMEM((PAIRS, ROWS), jnp.float32),
            pltpu.VMEM((PAIRS, ROWS), jnp.float32),
            pltpu.SMEM((Z,), jnp.int32),
            pltpu.VMEM((Z + 1, GROUP * ROWS, 2 * ROWS), jnp.float32),
            pltpu.VMEM((GROUP * ROWS, ROWS), jnp.float32),
            pltpu.VMEM((GROUP * ROWS, 2 * HEAD_DIM), jnp.float32),
        ],
        compiler_params=params,
        cost_estimate=pl.CostEstimate(
            flops=16_000_000_000, bytes_accessed=6_000_000, transcendentals=4_000_000
        ),
        name="attention",
    )(query, own, other, prev_own, prev_other_0, prev_other_1)

    attn, far1, near2, near3 = lax.optimization_barrier((attn, far1, near2, near3))
    far2, far3 = x_down(near2[1]), x_up(near3[0])
    weights = (
        group1, group2, group3,
        near1[0], near2[0], near3[0],
        near1[1], near2[1], near3[1],
        far1, far2, far3,
    )
    spread = lax.all_to_all(attn, ("zh", "zl", "core", "yl"), 0, 0, tiled=True)
    one = jax.ShapeDtypeStruct((ROWS, cols), bf16)
    two = jax.ShapeDtypeStruct((2, ROWS, cols), bf16)
    f32 = jnp.float32
    parts = []
    for j in range(HALVES):
        keep, send, theirs = pl.pallas_call(
            projection_kernel,
            grid=(1,),
            in_specs=[pl.BlockSpec(memory_space=pltpu.VMEM)]
            + [
                pl.BlockSpec((w.shape[0], ROWS, cols // 4), functools.partial(column_half, j))
                for w in weights
            ],
            out_shape=[one, one, two],
            scratch_shapes=[pltpu.VMEM((4 * ROWS, Z * ROWS), bf16)],
            compiler_params=params,
            cost_estimate=pl.CostEstimate(
                flops=2 * 4 * ROWS * Z * ROWS * cols,
                bytes_accessed=2 * Z * ROWS * cols + 8 * ROWS * cols,
                transcendentals=0,
            ),
            name="projection",
        )(spread, *weights)
        arrived = lax.ppermute(theirs, "core", swap)
        send = (send.astype(f32) + arrived[1].astype(f32)).astype(bf16)
        if j + 1 < HALVES:
            spread, send = lax.optimization_barrier((spread, send))
        parts += (keep, arrived, lax.ppermute(send, "yl", swap))
    return pl.pallas_call(
        finish_kernel,
        out_shape=jax.ShapeDtypeStruct((ROWS, out_cols), bf16),
        compiler_params=params,
        name="finish",
    )(*parts)


def solution(mesh):
    torus = Mesh(mesh.devices.reshape(4, 2, 2, 4, 2, 2), AXES)
    uly = ("zh", "zl", "yh")
    rows = P(BLK + uly, None)
    in_specs = (rows, rows, rows, P(BLK + uly), P(uly, None))
    return jax.shard_map(body, mesh=torus, in_specs=in_specs, out_specs=rows, check_vma=False)
```

```python
import functools
import math

import jax
import jax.numpy as jnp
from jax import lax
from jax.experimental import pallas as pl
from jax.experimental.pallas import tpu as pltpu
from jax.sharding import Mesh
from jax.sharding import PartitionSpec as P

HEAD_DIM = 128
ROWS = 128
Z = 8
GROUP = 4
PAIRS = 16
EXP2_SCALE = math.log2(math.e) / math.sqrt(HEAD_DIM)
MASKED = -1e30
MIB = 1024 * 1024

AXES = ("x", "yl", "core", "zh", "zl", "yh")
BLK = ("x", "yl", "core")


def pack_kernel(k_ref, v_ref, id_ref, o_ref):
    ids = jnp.broadcast_to((id_ref[...] + 1).astype(jnp.float32), (16, ROWS)).astype(jnp.bfloat16)
    for g in range(Z):
        cols = slice(g * HEAD_DIM, (g + 1) * HEAD_DIM)
        o_ref[g, 0:ROWS, 0:HEAD_DIM] = k_ref[:, cols]
        o_ref[g, 0:ROWS, HEAD_DIM : 2 * HEAD_DIM] = v_ref[:, cols]
        o_ref[g, ROWS : ROWS + 16, 0:HEAD_DIM] = ids
        o_ref[g, ROWS : ROWS + 16, HEAD_DIM : 2 * HEAD_DIM] = ids


def attention_kernel(
    q_ref, own_ref, oth_ref, pown_ref, poth0_ref, poth1_ref, o_ref,
    k_buf, v_buf, ids_own, ids_oth, last_ref, lo_ref, s_ref, m_ref, acc_ref,
):
    odd = lax.axis_index("yh") == 1
    ones = jnp.ones((2 * ROWS, HEAD_DIM), jnp.bfloat16)
    for side, (a, b) in enumerate((((pown_ref,), (poth0_ref, poth1_ref)), ((own_ref,), (oth_ref,)))):
        for g in range(Z):
            p = side * Z + g
            for half, parts in enumerate((a, b)):
                block = parts[0][g] if len(parts) == 1 else parts[0][g] + parts[1][g]
                rows = slice(half * ROWS, (half + 1) * ROWS)
                k_buf[p, rows, :] = block[0:ROWS, 0:HEAD_DIM]
                v_buf[p, rows, 0:HEAD_DIM] = block[0:ROWS, HEAD_DIM : 2 * HEAD_DIM]
                ids = block[ROWS : ROWS + 16, 0:HEAD_DIM].astype(jnp.float32)[0:1, :]
                (ids_own if half == 0 else ids_oth)[p : p + 1, :] = ids
            v_buf[p, :, HEAD_DIM : 2 * HEAD_DIM] = ones
    last_ref[...] = jnp.broadcast_to(
        jnp.max(jnp.maximum(ids_own[...], ids_oth[...]), axis=1, keepdims=True), (PAIRS, ROWS)
    )
    for z in range(Z):
        first = jnp.min(ids_own[Z + z : Z + z + 1, :], axis=1, keepdims=True)
        before = jnp.where(last_ref[...] < first, 1.0 / ROWS, 0.0)
        lo_ref[z] = jnp.sum(before).astype(jnp.int32)

    def scores(q4, p):
        return lax.dot_general(
            q4, k_buf[p], (((1,), (1,)), ((), ())), preferred_element_type=jnp.float32
        )

    def weigh(slot, p):
        part = s_ref[slot]
        peak = jnp.concatenate([m_ref[...]] * 2, axis=1)
        weights = jnp.exp2((part - peak) * EXP2_SCALE).astype(jnp.bfloat16)
        return jnp.dot(weights, v_buf[p], preferred_element_type=jnp.float32)

    @pl.loop(0, Z)
    def _(z):
        q = q_ref[z]
        q4 = jnp.concatenate([q[:, g * HEAD_DIM : (g + 1) * HEAD_DIM] for g in range(GROUP)], axis=0)
        diag = Z + z
        count = jnp.clip(diag - lo_ref[z], 0, Z)
        steps = (count + 1) // 2
        qid = jnp.transpose(jnp.broadcast_to(ids_own[pl.ds(diag, 1), :], (ROWS, ROWS)))

        def put(slot, part, keep_own, keep_oth, start):
            for g in range(GROUP):
                rows = slice(g * ROWS, (g + 1) * ROWS)
                left = jnp.where(keep_own, part[rows, 0:ROWS], MASKED)
                right = jnp.where(keep_oth, part[rows, ROWS : 2 * ROWS], MASKED)
                s_ref[slot, rows, 0:ROWS] = left
                s_ref[slot, rows, ROWS : 2 * ROWS] = right
                most = jnp.maximum(left, right)
                m_ref[rows, :] = most if start else jnp.maximum(m_ref[rows, :], most)

        at_row = lax.broadcasted_iota(jnp.int32, (ROWS, ROWS), 0)
        at_col = lax.broadcasted_iota(jnp.int32, (ROWS, ROWS), 1)
        same_own = ids_own[pl.ds(diag, 1), :] == qid
        same_oth = ids_oth[pl.ds(diag, 1), :] == qid
        put(Z, scores(q4, diag), same_own & (at_col <= at_row), same_oth & odd, True)

        @pl.loop(0, steps)
        def _(k):
            for u in range(2):
                slot = 2 * k + u
                p = jnp.maximum(diag - 1 - slot, 0)
                put(
                    slot,
                    scores(q4, p),
                    ids_own[pl.ds(p, 1), :] == qid,
                    ids_oth[pl.ds(p, 1), :] == qid,
                    False,
                )

        m_ref[...] = jnp.broadcast_to(
            jnp.max(m_ref[...], axis=1, keepdims=True), (GROUP * ROWS, ROWS)
        )
        acc_ref[...] = weigh(Z, diag)

        @pl.loop(0, steps)
        def _(k):
            total = None
            for u in range(2):
                slot = 2 * k + u
                p = jnp.maximum(diag - 1 - slot, 0)
                term = weigh(slot, p)
                total = term if total is None else total + term
            acc_ref[...] += total

        for g in range(GROUP):
            rows = slice(g * ROWS, (g + 1) * ROWS)
            out = acc_ref[rows, 0:HEAD_DIM] / acc_ref[rows, HEAD_DIM : 2 * HEAD_DIM]
            o_ref[4 * z + 2 * (g % 2) + g // 2] = out.astype(jnp.bfloat16)


def projection_kernel(spread_ref, *refs):
    w_refs, (keep_ref, send_ref, other_ref, a_buf) = refs[:-4], refs[-4:]
    core = lax.axis_index("core")
    yl = lax.axis_index("yl")
    for t in range(2):
        for u in range(2):
            source = 2 * (core if t == 0 else 1 - core) + (yl if u == 0 else 1 - yl)
            at = (2 * t + u) * ROWS
            for z in range(Z):
                a_buf[at : at + ROWS, z * ROWS : (z + 1) * ROWS] = spread_ref[4 * z + source]
    at = 0
    for ref in w_refs:
        y, done = None, 0
        for part in ref if isinstance(ref, tuple) else (ref,):
            depth = part.shape[0] * ROWS
            term = jnp.dot(
                a_buf[:, done : done + depth],
                part[...].reshape(depth, part.shape[-1]),
                preferred_element_type=jnp.float32,
            )
            y, done = (term if y is None else y + term), done + depth
        y = y.astype(jnp.bfloat16)
        cols = slice(at, at + y.shape[1])
        at += y.shape[1]
        keep_ref[:, cols] = y[0:ROWS]
        send_ref[:, cols] = y[ROWS : 2 * ROWS]
        for u in range(2):
            other_ref[u, :, cols] = y[(2 + u) * ROWS : (3 + u) * ROWS]


def far_kernel(spread_ref, low_ref, high_ref, *refs):
    projection_kernel(spread_ref, (low_ref, high_ref), *refs)


def finish_kernel(*refs):
    o_ref = refs[-1]
    piece = o_ref.shape[-1] // 4
    x = lax.axis_index("x")
    for n, shift in enumerate((0, 3, 1, 2)):
        keep, arrived, last = refs[0:3] if n < 3 else refs[3:6]
        cols = slice((n % 3) * piece, (n % 3 + 1) * piece)
        total = keep[:, cols].astype(jnp.float32) + arrived[0, :, cols].astype(jnp.float32)
        total = total + last[:, cols].astype(jnp.float32)
        at = pl.multiple_of(lax.rem(x + shift, 4) * piece, piece)
        o_ref[:, pl.ds(at, piece)] = total.astype(jnp.bfloat16)


def body(queries, keys, values, doc_ids, out_weight):
    bf16 = jnp.bfloat16
    def params(mib):
        return pltpu.CompilerParams(vmem_limit_bytes=mib * MIB)

    core = lax.axis_index("core")
    out_cols = out_weight.shape[1]
    swap = [(0, 1), (1, 0)]

    packed = pl.pallas_call(
        pack_kernel,
        out_shape=jax.ShapeDtypeStruct((Z, ROWS + 16, 2 * HEAD_DIM), bf16),
        compiler_params=params(8),
        name="pack_kv",
    )(keys, values, doc_ids.reshape(1, ROWS))
    def ring(axis, size, step):
        return lambda a: lax.ppermute(a, axis, [(i, (i + step) % size) for i in range(size)])

    x_up, x_down = ring("x", 4, 1), ring("x", 4, -1)

    piece = lax.dynamic_slice(
        out_weight, (core * ROWS, lax.axis_index("x") * (out_cols // 4)), (ROWS, out_cols // 4)
    )
    piece = lax.ppermute(piece, ("yl", "yh"), [(0, 0), (1, 2), (2, 1), (3, 3)])
    piece, packed = lax.optimization_barrier((piece, packed))
    own = lax.all_to_all(packed, ("zh", "zl"), 0, 0, tiled=True)
    here = lax.all_gather(piece, ("zh", "zl"), axis=0, tiled=False)
    other = lax.ppermute(own, "yh", swap)
    prev_own = lax.ppermute(own, BLK, [(i, i + 1) for i in range(15)])
    prev_other_0 = lax.ppermute(
        own,
        BLK + ("yh",),
        [(2 * i + h, 2 * (i + 1) + 1 - h) for i in range(1, 15, 2) for h in range(2)],
    )
    prev_other_1 = lax.ppermute(other, "core", [(0, 1)])

    split = queries.reshape(ROWS, Z, GROUP * HEAD_DIM).transpose(1, 0, 2)
    query = lax.all_to_all(split, ("zh", "zl"), 0, 0, tiled=True)
    query, here = lax.optimization_barrier((query, here))
    before, after = x_up(here), x_down(here)
    attn = pl.pallas_call(
        attention_kernel,
        out_shape=jax.ShapeDtypeStruct((4 * Z, ROWS, HEAD_DIM), bf16),
        scratch_shapes=[
            pltpu.VMEM((PAIRS, 2 * ROWS, HEAD_DIM), bf16),
            pltpu.VMEM((PAIRS, 2 * ROWS, 2 * HEAD_DIM), bf16),
            pltpu.VMEM((PAIRS, ROWS), jnp.float32),
            pltpu.VMEM((PAIRS, ROWS), jnp.float32),
            pltpu.VMEM((PAIRS, ROWS), jnp.float32),
            pltpu.SMEM((Z,), jnp.int32),
            pltpu.VMEM((Z + 1, GROUP * ROWS, 2 * ROWS), jnp.float32),
            pltpu.VMEM((GROUP * ROWS, ROWS), jnp.float32),
            pltpu.VMEM((GROUP * ROWS, 2 * HEAD_DIM), jnp.float32),
        ],
        compiler_params=params(24),
        cost_estimate=pl.CostEstimate(
            flops=16_000_000_000, bytes_accessed=6_000_000, transcendentals=4_000_000
        ),
        name="attention",
    )(query, own, other, prev_own, prev_other_0, prev_other_1)

    spread = lax.all_to_all(attn, ("zh", "zl", "core", "yl"), 0, 0, tiled=True)
    far_low, far_high = x_up(before[: Z // 2]), x_down(after[Z // 2 :])
    f32 = jnp.float32
    parts = []
    for kernel, weights, blocks in (
        (projection_kernel, (here, before, after), 3),
        (far_kernel, (far_low, far_high), 1),
    ):
        cols = blocks * out_cols // 4
        if parts:
            spread, parts[2] = lax.optimization_barrier((spread, parts[2]))
            parts[2] = lax.ppermute(parts[2], "yl", swap)
        one = jax.ShapeDtypeStruct((ROWS, cols), bf16)
        keep, send, theirs = pl.pallas_call(
            kernel,
            out_shape=[one, one, jax.ShapeDtypeStruct((2, ROWS, cols), bf16)],
            scratch_shapes=[pltpu.VMEM((4 * ROWS, Z * ROWS), bf16)],
            compiler_params=params(40),
            cost_estimate=pl.CostEstimate(
                flops=2 * 4 * ROWS * Z * ROWS * cols,
                bytes_accessed=2 * Z * ROWS * cols + 8 * ROWS * cols,
                transcendentals=0,
            ),
            name="projection",
        )(spread, *weights)
        arrived = lax.ppermute(theirs, "core", swap)
        parts += [keep, arrived, (send.astype(f32) + arrived[1].astype(f32)).astype(bf16)]
    parts[5] = lax.ppermute(parts[5], "yl", swap)
    return pl.pallas_call(
        finish_kernel,
        out_shape=jax.ShapeDtypeStruct((ROWS, out_cols), bf16),
        compiler_params=params(16),
        name="finish",
    )(*parts)


def solution(mesh):
    torus = Mesh(mesh.devices.reshape(4, 2, 2, 4, 2, 2), AXES)
    uly = ("zh", "zl", "yh")
    rows = P(BLK + uly, None)
    in_specs = (rows, rows, rows, P(BLK + uly), P(uly, None))
    return jax.shard_map(body, mesh=torus, in_specs=in_specs, out_specs=rows, check_vma=False)
```

```python
import functools
import math

import jax
import jax.numpy as jnp
from jax import lax
from jax.experimental import pallas as pl
from jax.experimental.pallas import tpu as pltpu
from jax.sharding import Mesh
from jax.sharding import PartitionSpec as P

HEAD_DIM = 128
ROWS = 128
Z = 8
GROUP = 4
PAIRS = 16
EXP2_SCALE = math.log2(math.e) / math.sqrt(HEAD_DIM)
MASKED = -1e30
MIB = 1024 * 1024

AXES = ("x", "yl", "core", "zh", "zl", "yh")
BLK = ("x", "yl", "core")


def pack_kernel(k_ref, v_ref, id_ref, o_ref):
    ids = jnp.broadcast_to((id_ref[...] + 1).astype(jnp.float32), (16, ROWS)).astype(jnp.bfloat16)
    for g in range(Z):
        cols = slice(g * HEAD_DIM, (g + 1) * HEAD_DIM)
        o_ref[g, 0:ROWS, 0:HEAD_DIM] = k_ref[:, cols]
        o_ref[g, 0:ROWS, HEAD_DIM : 2 * HEAD_DIM] = v_ref[:, cols]
        o_ref[g, ROWS : ROWS + 16, 0:HEAD_DIM] = ids
        o_ref[g, ROWS : ROWS + 16, HEAD_DIM : 2 * HEAD_DIM] = ids


def attention_kernel(
    q_ref, own_ref, oth_ref, pown_ref, poth0_ref, poth1_ref, o_ref,
    k_buf, v_buf, ids_own, ids_oth, last_ref, lo_ref, s_ref, m_ref, acc_ref,
):
    odd = lax.axis_index("yh") == 1
    ones = jnp.ones((2 * ROWS, HEAD_DIM), jnp.bfloat16)
    for side, (a, b) in enumerate((((pown_ref,), (poth0_ref, poth1_ref)), ((own_ref,), (oth_ref,)))):
        for g in range(Z):
            p = side * Z + g
            for half, parts in enumerate((a, b)):
                block = parts[0][g] if len(parts) == 1 else parts[0][g] + parts[1][g]
                rows = slice(half * ROWS, (half + 1) * ROWS)
                k_buf[p, rows, :] = block[0:ROWS, 0:HEAD_DIM]
                v_buf[p, rows, 0:HEAD_DIM] = block[0:ROWS, HEAD_DIM : 2 * HEAD_DIM]
                ids = block[ROWS : ROWS + 16, 0:HEAD_DIM].astype(jnp.float32)[0:1, :]
                (ids_own if half == 0 else ids_oth)[p : p + 1, :] = ids
            v_buf[p, :, HEAD_DIM : 2 * HEAD_DIM] = ones
    last_ref[...] = jnp.broadcast_to(
        jnp.max(jnp.maximum(ids_own[...], ids_oth[...]), axis=1, keepdims=True), (PAIRS, ROWS)
    )
    for z in range(Z):
        first = jnp.min(ids_own[Z + z : Z + z + 1, :], axis=1, keepdims=True)
        before = jnp.where(last_ref[...] < first, 1.0 / ROWS, 0.0)
        lo_ref[z] = jnp.sum(before).astype(jnp.int32)

    def scores(q4, p):
        return lax.dot_general(
            q4, k_buf[p], (((1,), (1,)), ((), ())), preferred_element_type=jnp.float32
        )

    def weigh(slot, p):
        part = s_ref[slot]
        peak = jnp.concatenate([m_ref[...]] * 2, axis=1)
        weights = jnp.exp2((part - peak) * EXP2_SCALE).astype(jnp.bfloat16)
        return jnp.dot(weights, v_buf[p], preferred_element_type=jnp.float32)

    @pl.loop(0, Z)
    def _(z):
        q = q_ref[z]
        q4 = jnp.concatenate([q[:, g * HEAD_DIM : (g + 1) * HEAD_DIM] for g in range(GROUP)], axis=0)
        diag = Z + z
        count = jnp.clip(diag - lo_ref[z], 0, Z)
        steps = (count + 1) // 2
        qid = jnp.transpose(jnp.broadcast_to(ids_own[pl.ds(diag, 1), :], (ROWS, ROWS)))

        def put(slot, part, keep_own, keep_oth, start):
            for g in range(GROUP):
                rows = slice(g * ROWS, (g + 1) * ROWS)
                left = jnp.where(keep_own, part[rows, 0:ROWS], MASKED)
                right = jnp.where(keep_oth, part[rows, ROWS : 2 * ROWS], MASKED)
                s_ref[slot, rows, 0:ROWS] = left
                s_ref[slot, rows, ROWS : 2 * ROWS] = right
                most = jnp.maximum(left, right)
                m_ref[rows, :] = most if start else jnp.maximum(m_ref[rows, :], most)

        at_row = lax.broadcasted_iota(jnp.int32, (ROWS, ROWS), 0)
        at_col = lax.broadcasted_iota(jnp.int32, (ROWS, ROWS), 1)
        same_own = ids_own[pl.ds(diag, 1), :] == qid
        same_oth = ids_oth[pl.ds(diag, 1), :] == qid
        put(Z, scores(q4, diag), same_own & (at_col <= at_row), same_oth & odd, True)

        @pl.loop(0, steps)
        def _(k):
            for u in range(2):
                slot = 2 * k + u
                p = jnp.maximum(diag - 1 - slot, 0)
                put(
                    slot,
                    scores(q4, p),
                    ids_own[pl.ds(p, 1), :] == qid,
                    ids_oth[pl.ds(p, 1), :] == qid,
                    False,
                )

        m_ref[...] = jnp.broadcast_to(
            jnp.max(m_ref[...], axis=1, keepdims=True), (GROUP * ROWS, ROWS)
        )
        acc_ref[...] = weigh(Z, diag)

        @pl.loop(0, steps)
        def _(k):
            total = None
            for u in range(2):
                slot = 2 * k + u
                p = jnp.maximum(diag - 1 - slot, 0)
                term = weigh(slot, p)
                total = term if total is None else total + term
            acc_ref[...] += total

        for g in range(GROUP):
            rows = slice(g * ROWS, (g + 1) * ROWS)
            out = acc_ref[rows, 0:HEAD_DIM] / acc_ref[rows, HEAD_DIM : 2 * HEAD_DIM]
            o_ref[4 * z + 2 * (g % 2) + g // 2] = out.astype(jnp.bfloat16)


def projection_kernel(spread_ref, *refs):
    w_refs, (keep_ref, send_ref, other_ref, a_buf) = refs[:-4], refs[-4:]
    core = lax.axis_index("core")
    yl = lax.axis_index("yl")
    x = lax.axis_index("x")
    for t in range(2):
        for u in range(2):
            source = 2 * (core if t == 0 else 1 - core) + (yl if u == 0 else 1 - yl)
            at = (2 * t + u) * ROWS
            for z in range(Z):
                a_buf[at : at + ROWS, z * ROWS : (z + 1) * ROWS] = spread_ref[4 * z + source]
    piece = w_refs[0].shape[-1]
    for shift, parts in ((0, w_refs[0:1]), (3, w_refs[1:3]), (1, w_refs[3:5]), (2, w_refs[5:7])):
        y, at = None, 0
        for part in parts:
            depth = part.shape[0] * ROWS
            w = part[...].reshape(depth, piece)
            term = jnp.dot(a_buf[:, at : at + depth], w, preferred_element_type=jnp.float32)
            y, at = (term if y is None else y + term), at + depth
        y = y.astype(jnp.bfloat16)
        cols = pl.ds(pl.multiple_of(lax.rem(x + shift, 4) * piece, piece), piece)
        keep_ref[:, cols] = y[0:ROWS]
        send_ref[:, cols] = y[ROWS : 2 * ROWS]
        for u in range(2):
            other_ref[u, :, cols] = y[(2 + u) * ROWS : (3 + u) * ROWS]


def finish_kernel(keep_ref, arrived_ref, last_ref, o_ref):
    total = keep_ref[...].astype(jnp.float32) + arrived_ref[0].astype(jnp.float32)
    o_ref[...] = (total + last_ref[...].astype(jnp.float32)).astype(jnp.bfloat16)


def body(queries, keys, values, doc_ids, out_weight):
    bf16 = jnp.bfloat16
    def params(mib):
        return pltpu.CompilerParams(vmem_limit_bytes=mib * MIB)

    core = lax.axis_index("core")
    out_cols = out_weight.shape[1]
    swap = [(0, 1), (1, 0)]

    packed = pl.pallas_call(
        pack_kernel,
        out_shape=jax.ShapeDtypeStruct((Z, ROWS + 16, 2 * HEAD_DIM), bf16),
        compiler_params=params(8),
        name="pack_kv",
    )(keys, values, doc_ids.reshape(1, ROWS))
    def ring(axis, size, step):
        return lambda a: lax.ppermute(a, axis, [(i, (i + step) % size) for i in range(size)])

    x_up, x_down = ring("x", 4, 1), ring("x", 4, -1)

    piece = lax.dynamic_slice(
        out_weight, (core * ROWS, lax.axis_index("x") * (out_cols // 4)), (ROWS, out_cols // 4)
    )
    piece = lax.ppermute(piece, ("yl", "yh"), [(0, 0), (1, 2), (2, 1), (3, 3)])
    piece, packed = lax.optimization_barrier((piece, packed))
    own = lax.all_to_all(packed, ("zh", "zl"), 0, 0, tiled=True)
    here = lax.all_gather(piece, ("zh", "zl"), axis=0, tiled=False)
    other = lax.ppermute(own, "yh", swap)
    prev_own = lax.ppermute(own, BLK, [(i, i + 1) for i in range(15)])
    prev_other_0 = lax.ppermute(
        own,
        BLK + ("yh",),
        [(2 * i + h, 2 * (i + 1) + 1 - h) for i in range(1, 15, 2) for h in range(2)],
    )
    prev_other_1 = lax.ppermute(other, "core", [(0, 1)])

    split = queries.reshape(ROWS, Z, GROUP * HEAD_DIM).transpose(1, 0, 2)
    split, here = lax.optimization_barrier((split, here))
    query = lax.all_to_all(split, ("zh", "zl"), 0, 0, tiled=True)
    before6, after6 = x_up(here[:6]), x_down(here[2:])
    query, before6, after6 = lax.optimization_barrier((query, before6, after6))
    before2, after2 = x_up(here[6:]), x_down(here[:2])
    attn = pl.pallas_call(
        attention_kernel,
        out_shape=jax.ShapeDtypeStruct((4 * Z, ROWS, HEAD_DIM), bf16),
        scratch_shapes=[
            pltpu.VMEM((PAIRS, 2 * ROWS, HEAD_DIM), bf16),
            pltpu.VMEM((PAIRS, 2 * ROWS, 2 * HEAD_DIM), bf16),
            pltpu.VMEM((PAIRS, ROWS), jnp.float32),
            pltpu.VMEM((PAIRS, ROWS), jnp.float32),
            pltpu.VMEM((PAIRS, ROWS), jnp.float32),
            pltpu.SMEM((Z,), jnp.int32),
            pltpu.VMEM((Z + 1, GROUP * ROWS, 2 * ROWS), jnp.float32),
            pltpu.VMEM((GROUP * ROWS, ROWS), jnp.float32),
            pltpu.VMEM((GROUP * ROWS, 2 * HEAD_DIM), jnp.float32),
        ],
        compiler_params=params(24),
        cost_estimate=pl.CostEstimate(
            flops=16_000_000_000, bytes_accessed=6_000_000, transcendentals=4_000_000
        ),
        name="attention",
    )(query, own, other, prev_own, prev_other_0, prev_other_1)

    attn, before2, after2 = lax.optimization_barrier((attn, before2, after2))
    far_low, far_high = x_up(before6[:4]), x_down(after6[2:])
    spread = lax.all_to_all(attn, ("zh", "zl", "core", "yl"), 0, 0, tiled=True)
    weights = (here, before6, before2, after2, after6, far_low, far_high)
    f32 = jnp.float32
    one = jax.ShapeDtypeStruct((ROWS, out_cols), bf16)
    keep, send, theirs = pl.pallas_call(
        projection_kernel,
        out_shape=[one, one, jax.ShapeDtypeStruct((2, ROWS, out_cols), bf16)],
        scratch_shapes=[pltpu.VMEM((4 * ROWS, Z * ROWS), bf16)],
        compiler_params=params(54),
        cost_estimate=pl.CostEstimate(
            flops=2 * 4 * ROWS * Z * ROWS * out_cols,
            bytes_accessed=2 * Z * ROWS * out_cols + 8 * ROWS * out_cols,
            transcendentals=0,
        ),
        name="projection",
    )(spread, *weights)
    arrived = lax.ppermute(theirs, "core", swap)
    last = lax.ppermute((send.astype(f32) + arrived[1].astype(f32)).astype(bf16), "yl", swap)
    return pl.pallas_call(
        finish_kernel,
        out_shape=one,
        compiler_params=params(16),
        name="finish",
    )(keep, arrived, last)


def solution(mesh):
    torus = Mesh(mesh.devices.reshape(4, 2, 2, 4, 2, 2), AXES)
    uly = ("zh", "zl", "yh")
    rows = P(BLK + uly, None)
    in_specs = (rows, rows, rows, P(BLK + uly), P(uly, None))
    return jax.shard_map(body, mesh=torus, in_specs=in_specs, out_specs=rows, check_vma=False)
```

```python
import functools
import math

import jax
import jax.numpy as jnp
from jax import lax
from jax.experimental import pallas as pl
from jax.experimental.pallas import tpu as pltpu
from jax.sharding import Mesh
from jax.sharding import PartitionSpec as P

HEAD_DIM = 128
ROWS = 128
Z = 8
GROUP = 4
PAIRS = 16
EXP2_SCALE = math.log2(math.e) / math.sqrt(HEAD_DIM)
MASKED = -1e30
MIB = 1024 * 1024

AXES = ("x", "yl", "core", "zh", "zl", "yh")
BLK = ("x", "yl", "core")


def pack_kernel(k_ref, v_ref, id_ref, o_ref):
    ids = jnp.broadcast_to((id_ref[...] + 1).astype(jnp.float32), (16, ROWS)).astype(jnp.bfloat16)
    for g in range(Z):
        cols = slice(g * HEAD_DIM, (g + 1) * HEAD_DIM)
        o_ref[g, 0:ROWS, 0:HEAD_DIM] = k_ref[:, cols]
        o_ref[g, 0:ROWS, HEAD_DIM : 2 * HEAD_DIM] = v_ref[:, cols]
        o_ref[g, ROWS : ROWS + 16, 0:HEAD_DIM] = ids
        o_ref[g, ROWS : ROWS + 16, HEAD_DIM : 2 * HEAD_DIM] = ids


def attention_kernel(
    q_ref, own_ref, oth_ref, pown_ref, poth0_ref, poth1_ref, o_ref,
    k_buf, v_buf, ids_own, ids_oth, last_ref, lo_ref, s_ref, m_ref, acc_ref,
):
    odd = lax.axis_index("yh") == 1
    ones = jnp.ones((2 * ROWS, HEAD_DIM), jnp.bfloat16)
    for side, (a, b) in enumerate((((pown_ref,), (poth0_ref, poth1_ref)), ((own_ref,), (oth_ref,)))):
        for g in range(Z):
            p = side * Z + g
            for half, parts in enumerate((a, b)):
                block = parts[0][g] if len(parts) == 1 else parts[0][g] + parts[1][g]
                rows = slice(half * ROWS, (half + 1) * ROWS)
                k_buf[p, rows, :] = block[0:ROWS, 0:HEAD_DIM]
                v_buf[p, rows, 0:HEAD_DIM] = block[0:ROWS, HEAD_DIM : 2 * HEAD_DIM]
                ids = block[ROWS : ROWS + 16, 0:HEAD_DIM].astype(jnp.float32)[0:1, :]
                (ids_own if half == 0 else ids_oth)[p : p + 1, :] = ids
            v_buf[p, :, HEAD_DIM : 2 * HEAD_DIM] = ones
    last_ref[...] = jnp.broadcast_to(
        jnp.max(jnp.maximum(ids_own[...], ids_oth[...]), axis=1, keepdims=True), (PAIRS, ROWS)
    )
    for z in range(Z):
        first = jnp.min(ids_own[Z + z : Z + z + 1, :], axis=1, keepdims=True)
        before = jnp.where(last_ref[...] < first, 1.0 / ROWS, 0.0)
        lo_ref[z] = jnp.sum(before).astype(jnp.int32)

    def scores(q4, p):
        return lax.dot_general(
            q4, k_buf[p], (((1,), (1,)), ((), ())), preferred_element_type=jnp.float32
        )

    def weigh(slot, p):
        part = s_ref[slot]
        peak = jnp.concatenate([m_ref[...]] * 2, axis=1)
        weights = jnp.exp2((part - peak) * EXP2_SCALE).astype(jnp.bfloat16)
        return jnp.dot(weights, v_buf[p], preferred_element_type=jnp.float32)

    @pl.loop(0, Z)
    def _(z):
        q = q_ref[z]
        q4 = jnp.concatenate([q[:, g * HEAD_DIM : (g + 1) * HEAD_DIM] for g in range(GROUP)], axis=0)
        diag = Z + z
        count = jnp.clip(diag - lo_ref[z], 0, Z)
        steps = (count + 1) // 2
        qid = jnp.transpose(jnp.broadcast_to(ids_own[pl.ds(diag, 1), :], (ROWS, ROWS)))

        def put(slot, part, keep_own, keep_oth, start):
            for g in range(GROUP):
                rows = slice(g * ROWS, (g + 1) * ROWS)
                left = jnp.where(keep_own, part[rows, 0:ROWS], MASKED)
                right = jnp.where(keep_oth, part[rows, ROWS : 2 * ROWS], MASKED)
                s_ref[slot, rows, 0:ROWS] = left
                s_ref[slot, rows, ROWS : 2 * ROWS] = right
                most = jnp.maximum(left, right)
                m_ref[rows, :] = most if start else jnp.maximum(m_ref[rows, :], most)

        at_row = lax.broadcasted_iota(jnp.int32, (ROWS, ROWS), 0)
        at_col = lax.broadcasted_iota(jnp.int32, (ROWS, ROWS), 1)
        same_own = ids_own[pl.ds(diag, 1), :] == qid
        same_oth = ids_oth[pl.ds(diag, 1), :] == qid
        put(Z, scores(q4, diag), same_own & (at_col <= at_row), same_oth & odd, True)

        @pl.loop(0, steps)
        def _(k):
            for u in range(2):
                slot = 2 * k + u
                p = jnp.maximum(diag - 1 - slot, 0)
                put(
                    slot,
                    scores(q4, p),
                    ids_own[pl.ds(p, 1), :] == qid,
                    ids_oth[pl.ds(p, 1), :] == qid,
                    False,
                )

        m_ref[...] = jnp.broadcast_to(
            jnp.max(m_ref[...], axis=1, keepdims=True), (GROUP * ROWS, ROWS)
        )
        acc_ref[...] = weigh(Z, diag)

        @pl.loop(0, steps)
        def _(k):
            total = None
            for u in range(2):
                slot = 2 * k + u
                p = jnp.maximum(diag - 1 - slot, 0)
                term = weigh(slot, p)
                total = term if total is None else total + term
            acc_ref[...] += total

        for g in range(GROUP):
            rows = slice(g * ROWS, (g + 1) * ROWS)
            out = acc_ref[rows, 0:HEAD_DIM] / acc_ref[rows, HEAD_DIM : 2 * HEAD_DIM]
            o_ref[4 * z + 2 * (g % 2) + g // 2] = out.astype(jnp.bfloat16)


def projection_kernel(spread_ref, *refs):
    w_refs, (keep_ref, send_ref, other_ref, a_buf) = refs[:-4], refs[-4:]
    step, steps = pl.program_id(0), pl.num_programs(0)
    x = lax.axis_index("x")

    @pl.when(step == 0)
    def _():
        core = lax.axis_index("core")
        yl = lax.axis_index("yl")
        for t in range(2):
            for u in range(2):
                source = 2 * (core if t == 0 else 1 - core) + (yl if u == 0 else 1 - yl)
                at = (2 * t + u) * ROWS
                for z in range(Z):
                    a_buf[at : at + ROWS, z * ROWS : (z + 1) * ROWS] = spread_ref[4 * z + source]

    half, piece = Z * ROWS // 2, w_refs[0].shape[-1]
    for n, shift in enumerate((0, 3, 1, 2)):
        low, high = (ref[...].reshape(half, piece) for ref in w_refs[2 * n : 2 * n + 2])
        y = jnp.dot(a_buf[:, 0:half], low, preferred_element_type=jnp.float32)
        y = y + jnp.dot(a_buf[:, half : 2 * half], high, preferred_element_type=jnp.float32)
        y = y.astype(jnp.bfloat16)
        block = lax.rem(x + shift, 4) * steps + step
        cols = pl.ds(pl.multiple_of(block * piece, piece), piece)
        keep_ref[:, cols] = y[0:ROWS]
        send_ref[:, cols] = y[ROWS : 2 * ROWS]
        for u in range(2):
            other_ref[u, :, cols] = y[(2 + u) * ROWS : (3 + u) * ROWS]


def finish_kernel(keep_ref, arrived_ref, last_ref, o_ref):
    total = keep_ref[...].astype(jnp.float32) + arrived_ref[0].astype(jnp.float32)
    o_ref[...] = (total + last_ref[...].astype(jnp.float32)).astype(jnp.bfloat16)


def body(queries, keys, values, doc_ids, out_weight):
    bf16 = jnp.bfloat16
    def params(mib):
        return pltpu.CompilerParams(vmem_limit_bytes=mib * MIB)

    core = lax.axis_index("core")
    out_cols = out_weight.shape[1]
    swap = [(0, 1), (1, 0)]

    packed = pl.pallas_call(
        pack_kernel,
        out_shape=jax.ShapeDtypeStruct((Z, ROWS + 16, 2 * HEAD_DIM), bf16),
        compiler_params=params(8),
        name="pack_kv",
    )(keys, values, doc_ids.reshape(1, ROWS))
    def ring(axis, size, step):
        return lambda a: lax.ppermute(a, axis, [(i, (i + step) % size) for i in range(size)])

    x_up, x_down = ring("x", 4, 1), ring("x", 4, -1)

    piece = lax.dynamic_slice(
        out_weight, (core * ROWS, lax.axis_index("x") * (out_cols // 4)), (ROWS, out_cols // 4)
    )
    piece = lax.ppermute(piece, ("yl", "yh"), [(0, 0), (1, 2), (2, 1), (3, 3)])
    piece, packed = lax.optimization_barrier((piece, packed))
    own = lax.all_to_all(packed, ("zh", "zl"), 0, 0, tiled=True)
    here = lax.all_gather(piece, ("zh", "zl"), axis=0, tiled=False)
    other = lax.ppermute(own, "yh", swap)
    prev_own = lax.ppermute(own, BLK, [(i, i + 1) for i in range(15)])
    prev_other_0 = lax.ppermute(
        own,
        BLK + ("yh",),
        [(2 * i + h, 2 * (i + 1) + 1 - h) for i in range(1, 15, 2) for h in range(2)],
    )
    prev_other_1 = lax.ppermute(other, "core", [(0, 1)])

    split = queries.reshape(ROWS, Z, GROUP * HEAD_DIM).transpose(1, 0, 2)
    query = lax.all_to_all(split, ("zh", "zl"), 0, 0, tiled=True)
    query, here = lax.optimization_barrier((query, here))
    low, high = here[: Z // 2], here[Z // 2 :]
    before_low, after_high = x_up(low), x_down(high)
    before_high, after_low = x_up(high), x_down(low)
    attn = pl.pallas_call(
        attention_kernel,
        out_shape=jax.ShapeDtypeStruct((4 * Z, ROWS, HEAD_DIM), bf16),
        scratch_shapes=[
            pltpu.VMEM((PAIRS, 2 * ROWS, HEAD_DIM), bf16),
            pltpu.VMEM((PAIRS, 2 * ROWS, 2 * HEAD_DIM), bf16),
            pltpu.VMEM((PAIRS, ROWS), jnp.float32),
            pltpu.VMEM((PAIRS, ROWS), jnp.float32),
            pltpu.VMEM((PAIRS, ROWS), jnp.float32),
            pltpu.SMEM((Z,), jnp.int32),
            pltpu.VMEM((Z + 1, GROUP * ROWS, 2 * ROWS), jnp.float32),
            pltpu.VMEM((GROUP * ROWS, ROWS), jnp.float32),
            pltpu.VMEM((GROUP * ROWS, 2 * HEAD_DIM), jnp.float32),
        ],
        compiler_params=params(24),
        cost_estimate=pl.CostEstimate(
            flops=16_000_000_000, bytes_accessed=6_000_000, transcendentals=4_000_000
        ),
        name="attention",
    )(query, own, other, prev_own, prev_other_0, prev_other_1)

    far_low, far_high = x_up(before_low), x_down(after_high)
    spread = lax.all_to_all(attn, ("zh", "zl", "core", "yl"), 0, 0, tiled=True)
    weights = (low, high, before_low, before_high, after_low, after_high, far_low, far_high)
    f32 = jnp.float32
    one = jax.ShapeDtypeStruct((ROWS, out_cols), bf16)
    steps = 4
    whole = pl.BlockSpec(memory_space=pltpu.VMEM)
    keep, send, theirs = pl.pallas_call(
        projection_kernel,
        grid=(steps,),
        in_specs=[whole]
        + [pl.BlockSpec((Z // 2, ROWS, out_cols // 4 // steps), lambda i: (0, 0, i))] * len(weights),
        out_specs=[whole] * 3,
        out_shape=[one, one, jax.ShapeDtypeStruct((2, ROWS, out_cols), bf16)],
        scratch_shapes=[pltpu.VMEM((4 * ROWS, Z * ROWS), bf16)],
        compiler_params=params(40),
        cost_estimate=pl.CostEstimate(
            flops=2 * 4 * ROWS * Z * ROWS * out_cols,
            bytes_accessed=2 * Z * ROWS * out_cols + 8 * ROWS * out_cols,
            transcendentals=0,
        ),
        name="projection",
    )(spread, *weights)
    arrived = lax.ppermute(theirs, "core", swap)
    last = lax.ppermute((send.astype(f32) + arrived[1].astype(f32)).astype(bf16), "yl", swap)
    return pl.pallas_call(
        finish_kernel,
        out_shape=one,
        compiler_params=params(16),
        name="finish",
    )(keep, arrived, last)


def solution(mesh):
    torus = Mesh(mesh.devices.reshape(4, 2, 2, 4, 2, 2), AXES)
    uly = ("zh", "zl", "yh")
    rows = P(BLK + uly, None)
    in_specs = (rows, rows, rows, P(BLK + uly), P(uly, None))
    return jax.shard_map(body, mesh=torus, in_specs=in_specs, out_specs=rows, check_vma=False)
```

```python
import functools
import math

import jax
import jax.numpy as jnp
from jax import lax
from jax.experimental import pallas as pl
from jax.experimental.pallas import tpu as pltpu
from jax.sharding import Mesh
from jax.sharding import PartitionSpec as P

HEAD_DIM = 128
ROWS = 128
Z = 8
GROUP = 4
PAIRS = 16
EXP2_SCALE = math.log2(math.e) / math.sqrt(HEAD_DIM)
MASKED = -1e30
MIB = 1024 * 1024

AXES = ("x", "yl", "core", "zh", "zl", "yh")
BLK = ("x", "yl", "core")


def pack_kernel(k_ref, v_ref, id_ref, o_ref):
    ids = jnp.broadcast_to((id_ref[...] + 1).astype(jnp.float32), (16, ROWS)).astype(jnp.bfloat16)
    for g in range(Z):
        cols = slice(g * HEAD_DIM, (g + 1) * HEAD_DIM)
        o_ref[g, 0:ROWS, 0:HEAD_DIM] = k_ref[:, cols]
        o_ref[g, 0:ROWS, HEAD_DIM : 2 * HEAD_DIM] = v_ref[:, cols]
        o_ref[g, ROWS : ROWS + 16, 0:HEAD_DIM] = ids
        o_ref[g, ROWS : ROWS + 16, HEAD_DIM : 2 * HEAD_DIM] = ids


def attention_kernel(
    q_ref, own_ref, oth_ref, pown_ref, poth0_ref, poth1_ref, o_ref,
    k_buf, v_buf, ids_own, ids_oth, last_ref, lo_ref, s_ref, m_ref, acc_ref,
):
    odd = lax.axis_index("yh") == 1
    ones = jnp.ones((2 * ROWS, HEAD_DIM), jnp.bfloat16)
    for side, (a, b) in enumerate((((pown_ref,), (poth0_ref, poth1_ref)), ((own_ref,), (oth_ref,)))):
        for g in range(Z):
            p = side * Z + g
            for half, parts in enumerate((a, b)):
                block = parts[0][g] if len(parts) == 1 else parts[0][g] + parts[1][g]
                rows = slice(half * ROWS, (half + 1) * ROWS)
                k_buf[p, rows, :] = block[0:ROWS, 0:HEAD_DIM]
                v_buf[p, rows, 0:HEAD_DIM] = block[0:ROWS, HEAD_DIM : 2 * HEAD_DIM]
                ids = block[ROWS : ROWS + 16, 0:HEAD_DIM].astype(jnp.float32)[0:1, :]
                (ids_own if half == 0 else ids_oth)[p : p + 1, :] = ids
            v_buf[p, :, HEAD_DIM : 2 * HEAD_DIM] = ones
    last_ref[...] = jnp.broadcast_to(
        jnp.max(jnp.maximum(ids_own[...], ids_oth[...]), axis=1, keepdims=True), (PAIRS, ROWS)
    )
    for z in range(Z):
        first = jnp.min(ids_own[Z + z : Z + z + 1, :], axis=1, keepdims=True)
        before = jnp.where(last_ref[...] < first, 1.0 / ROWS, 0.0)
        lo_ref[z] = jnp.sum(before).astype(jnp.int32)

    def scores(q4, p):
        return lax.dot_general(
            q4, k_buf[p], (((1,), (1,)), ((), ())), preferred_element_type=jnp.float32
        )

    def weigh(slot, p):
        part = s_ref[slot]
        peak = jnp.concatenate([m_ref[...]] * 2, axis=1)
        weights = jnp.exp2((part - peak) * EXP2_SCALE).astype(jnp.bfloat16)
        return jnp.dot(weights, v_buf[p], preferred_element_type=jnp.float32)

    @pl.loop(0, Z)
    def _(z):
        q = q_ref[z]
        q4 = jnp.concatenate([q[:, g * HEAD_DIM : (g + 1) * HEAD_DIM] for g in range(GROUP)], axis=0)
        diag = Z + z
        count = jnp.clip(diag - lo_ref[z], 0, Z)
        steps = (count + 1) // 2
        qid = jnp.transpose(jnp.broadcast_to(ids_own[pl.ds(diag, 1), :], (ROWS, ROWS)))

        def put(slot, part, keep_own, keep_oth, start):
            for g in range(GROUP):
                rows = slice(g * ROWS, (g + 1) * ROWS)
                left = jnp.where(keep_own, part[rows, 0:ROWS], MASKED)
                right = jnp.where(keep_oth, part[rows, ROWS : 2 * ROWS], MASKED)
                s_ref[slot, rows, 0:ROWS] = left
                s_ref[slot, rows, ROWS : 2 * ROWS] = right
                most = jnp.maximum(left, right)
                m_ref[rows, :] = most if start else jnp.maximum(m_ref[rows, :], most)

        at_row = lax.broadcasted_iota(jnp.int32, (ROWS, ROWS), 0)
        at_col = lax.broadcasted_iota(jnp.int32, (ROWS, ROWS), 1)
        same_own = ids_own[pl.ds(diag, 1), :] == qid
        same_oth = ids_oth[pl.ds(diag, 1), :] == qid
        put(Z, scores(q4, diag), same_own & (at_col <= at_row), same_oth & odd, True)

        @pl.loop(0, steps)
        def _(k):
            for u in range(2):
                slot = 2 * k + u
                p = jnp.maximum(diag - 1 - slot, 0)
                put(
                    slot,
                    scores(q4, p),
                    ids_own[pl.ds(p, 1), :] == qid,
                    ids_oth[pl.ds(p, 1), :] == qid,
                    False,
                )

        m_ref[...] = jnp.broadcast_to(
            jnp.max(m_ref[...], axis=1, keepdims=True), (GROUP * ROWS, ROWS)
        )
        acc_ref[...] = weigh(Z, diag)

        @pl.loop(0, steps)
        def _(k):
            total = None
            for u in range(2):
                slot = 2 * k + u
                p = jnp.maximum(diag - 1 - slot, 0)
                term = weigh(slot, p)
                total = term if total is None else total + term
            acc_ref[...] += total

        for g in range(GROUP):
            rows = slice(g * ROWS, (g + 1) * ROWS)
            out = acc_ref[rows, 0:HEAD_DIM] / acc_ref[rows, HEAD_DIM : 2 * HEAD_DIM]
            o_ref[4 * z + 2 * (g % 2) + g // 2] = out.astype(jnp.bfloat16)


def projection_kernel(spread_ref, *refs):
    w_refs, (keep_ref, send_ref, other_ref, a_buf) = refs[:-4], refs[-4:]
    core = lax.axis_index("core")
    yl = lax.axis_index("yl")
    for t in range(2):
        for u in range(2):
            source = 2 * (core if t == 0 else 1 - core) + (yl if u == 0 else 1 - yl)
            at = (2 * t + u) * ROWS
            for z in range(Z):
                a_buf[at : at + ROWS, z * ROWS : (z + 1) * ROWS] = spread_ref[4 * z + source]
    at = 0
    for ref in w_refs:
        y, done = None, 0
        for part in ref if isinstance(ref, tuple) else (ref,):
            depth = part.shape[0] * ROWS
            term = jnp.dot(
                a_buf[:, done : done + depth],
                part[...].reshape(depth, part.shape[-1]),
                preferred_element_type=jnp.float32,
            )
            y, done = (term if y is None else y + term), done + depth
        y = y.astype(jnp.bfloat16)
        cols = slice(at, at + y.shape[1])
        at += y.shape[1]
        keep_ref[:, cols] = y[0:ROWS]
        send_ref[:, cols] = y[ROWS : 2 * ROWS]
        for u in range(2):
            other_ref[u, :, cols] = y[(2 + u) * ROWS : (3 + u) * ROWS]


def far_kernel(spread_ref, *refs):
    projection_kernel(spread_ref, refs[:4], *refs[4:])


def finish_kernel(*refs):
    o_ref = refs[-1]
    piece = o_ref.shape[-1] // 4
    x = lax.axis_index("x")
    for n, shift in enumerate((0, 3, 1, 2)):
        keep, arrived, last = refs[0:3] if n < 3 else refs[3:6]
        cols = slice((n % 3) * piece, (n % 3 + 1) * piece)
        total = keep[:, cols].astype(jnp.float32) + arrived[0, :, cols].astype(jnp.float32)
        total = total + last[:, cols].astype(jnp.float32)
        at = pl.multiple_of(lax.rem(x + shift, 4) * piece, piece)
        o_ref[:, pl.ds(at, piece)] = total.astype(jnp.bfloat16)


def body(queries, keys, values, doc_ids, out_weight):
    bf16 = jnp.bfloat16
    def params(mib):
        return pltpu.CompilerParams(vmem_limit_bytes=mib * MIB)

    core = lax.axis_index("core")
    out_cols = out_weight.shape[1]
    swap = [(0, 1), (1, 0)]

    packed = pl.pallas_call(
        pack_kernel,
        out_shape=jax.ShapeDtypeStruct((Z, ROWS + 16, 2 * HEAD_DIM), bf16),
        compiler_params=params(8),
        name="pack_kv",
    )(keys, values, doc_ids.reshape(1, ROWS))
    def ring(axis, size, step):
        return lambda a: lax.ppermute(a, axis, [(i, (i + step) % size) for i in range(size)])

    x_up, x_down = ring("x", 4, 1), ring("x", 4, -1)

    piece = lax.dynamic_slice(
        out_weight, (core * ROWS, lax.axis_index("x") * (out_cols // 4)), (ROWS, out_cols // 4)
    )
    piece = lax.ppermute(piece, ("yl", "yh"), [(0, 0), (1, 2), (2, 1), (3, 3)])
    piece, packed = lax.optimization_barrier((piece, packed))
    own = lax.all_to_all(packed, ("zh", "zl"), 0, 0, tiled=True)
    here = lax.all_gather(piece, ("zh", "zl"), axis=0, tiled=False)
    other = lax.ppermute(own, "yh", swap)
    prev_own = lax.ppermute(own, BLK, [(i, i + 1) for i in range(15)])
    prev_other_0 = lax.ppermute(
        own,
        BLK + ("yh",),
        [(2 * i + h, 2 * (i + 1) + 1 - h) for i in range(1, 15, 2) for h in range(2)],
    )
    prev_other_1 = lax.ppermute(other, "core", [(0, 1)])

    split = queries.reshape(ROWS, Z, GROUP * HEAD_DIM).transpose(1, 0, 2)
    query = lax.all_to_all(split, ("zh", "zl"), 0, 0, tiled=True)
    query, here = lax.optimization_barrier((query, here))
    before, after = x_up(here), x_down(here)
    attn = pl.pallas_call(
        attention_kernel,
        out_shape=jax.ShapeDtypeStruct((4 * Z, ROWS, HEAD_DIM), bf16),
        scratch_shapes=[
            pltpu.VMEM((PAIRS, 2 * ROWS, HEAD_DIM), bf16),
            pltpu.VMEM((PAIRS, 2 * ROWS, 2 * HEAD_DIM), bf16),
            pltpu.VMEM((PAIRS, ROWS), jnp.float32),
            pltpu.VMEM((PAIRS, ROWS), jnp.float32),
            pltpu.VMEM((PAIRS, ROWS), jnp.float32),
            pltpu.SMEM((Z,), jnp.int32),
            pltpu.VMEM((Z + 1, GROUP * ROWS, 2 * ROWS), jnp.float32),
            pltpu.VMEM((GROUP * ROWS, ROWS), jnp.float32),
            pltpu.VMEM((GROUP * ROWS, 2 * HEAD_DIM), jnp.float32),
        ],
        compiler_params=params(24),
        cost_estimate=pl.CostEstimate(
            flops=16_000_000_000, bytes_accessed=6_000_000, transcendentals=4_000_000
        ),
        name="attention",
    )(query, own, other, prev_own, prev_other_0, prev_other_1)

    spread = lax.all_to_all(attn, ("zh", "zl", "core", "yl"), 0, 0, tiled=True)
    far1 = x_up(before[:1]), x_down(after[4:5])
    spread, far1 = lax.optimization_barrier((spread, far1))
    far2 = x_up(before[1:4]), x_down(after[5:])
    far = far1[0], far2[0], far1[1], far2[1]
    f32 = jnp.float32
    parts = []
    for kernel, weights, blocks in (
        (projection_kernel, (here, before, after), 3),
        (far_kernel, far, 1),
    ):
        cols = blocks * out_cols // 4
        if parts:
            parts[2] = lax.ppermute(parts[2], "yl", swap)
            spread, parts[2] = lax.optimization_barrier((spread, parts[2]))
        one = jax.ShapeDtypeStruct((ROWS, cols), bf16)
        keep, send, theirs = pl.pallas_call(
            kernel,
            out_shape=[one, one, jax.ShapeDtypeStruct((2, ROWS, cols), bf16)],
            scratch_shapes=[pltpu.VMEM((4 * ROWS, Z * ROWS), bf16)],
            compiler_params=params(40),
            cost_estimate=pl.CostEstimate(
                flops=2 * 4 * ROWS * Z * ROWS * cols,
                bytes_accessed=2 * Z * ROWS * cols + 8 * ROWS * cols,
                transcendentals=0,
            ),
            name="projection",
        )(spread, *weights)
        arrived = lax.ppermute(theirs, "core", swap)
        parts += [keep, arrived, (send.astype(f32) + arrived[1].astype(f32)).astype(bf16)]
    parts[5] = lax.ppermute(parts[5], "yl", swap)
    return pl.pallas_call(
        finish_kernel,
        out_shape=jax.ShapeDtypeStruct((ROWS, out_cols), bf16),
        compiler_params=params(16),
        name="finish",
    )(*parts)


def solution(mesh):
    torus = Mesh(mesh.devices.reshape(4, 2, 2, 4, 2, 2), AXES)
    uly = ("zh", "zl", "yh")
    rows = P(BLK + uly, None)
    in_specs = (rows, rows, rows, P(BLK + uly), P(uly, None))
    return jax.shard_map(body, mesh=torus, in_specs=in_specs, out_specs=rows, check_vma=False)
```

```python
import functools
import math

import jax
import jax.numpy as jnp
from jax import lax
from jax.experimental import pallas as pl
from jax.experimental.pallas import tpu as pltpu
from jax.sharding import Mesh
from jax.sharding import PartitionSpec as P

HEAD_DIM = 128
ROWS = 128
Z = 8
GROUP = 4
PAIRS = 16
EXP2_SCALE = math.log2(math.e) / math.sqrt(HEAD_DIM)
MASKED = -1e30
Z_ORDER = (0, 7, 1, 2, 3, 4, 5, 6)
MIB = 1024 * 1024

AXES = ("x", "yl", "core", "zh", "zl", "yh")
BLK = ("x", "yl", "core")


def pack_kernel(k_ref, v_ref, id_ref, o_ref):
    ids = jnp.broadcast_to((id_ref[...] + 1).astype(jnp.float32), (16, ROWS)).astype(jnp.bfloat16)
    for g in range(Z):
        cols = slice(g * HEAD_DIM, (g + 1) * HEAD_DIM)
        o_ref[g, 0:ROWS, 0:HEAD_DIM] = k_ref[:, cols]
        o_ref[g, 0:ROWS, HEAD_DIM : 2 * HEAD_DIM] = v_ref[:, cols]
        o_ref[g, ROWS : ROWS + 16, 0:HEAD_DIM] = ids
        o_ref[g, ROWS : ROWS + 16, HEAD_DIM : 2 * HEAD_DIM] = ids


def attention_kernel(
    q_ref, own_ref, oth_ref, pown_ref, poth0_ref, poth1_ref, o_ref,
    k_buf, v_buf, ids_own, ids_oth, last_ref, lo_ref, s_ref, m_ref, acc_ref,
):
    odd = lax.axis_index("yh") == 1
    ones = jnp.ones((2 * ROWS, HEAD_DIM), jnp.bfloat16)
    for side, (a, b) in enumerate((((pown_ref,), (poth0_ref, poth1_ref)), ((own_ref,), (oth_ref,)))):
        for g in range(Z):
            p = side * Z + g
            for half, parts in enumerate((a, b)):
                block = parts[0][g] if len(parts) == 1 else parts[0][g] + parts[1][g]
                rows = slice(half * ROWS, (half + 1) * ROWS)
                k_buf[p, rows, :] = block[0:ROWS, 0:HEAD_DIM]
                v_buf[p, rows, 0:HEAD_DIM] = block[0:ROWS, HEAD_DIM : 2 * HEAD_DIM]
                ids = block[ROWS : ROWS + 16, 0:HEAD_DIM].astype(jnp.float32)[0:1, :]
                (ids_own if half == 0 else ids_oth)[p : p + 1, :] = ids
            v_buf[p, :, HEAD_DIM : 2 * HEAD_DIM] = ones
    last_ref[...] = jnp.broadcast_to(
        jnp.max(jnp.maximum(ids_own[...], ids_oth[...]), axis=1, keepdims=True), (PAIRS, ROWS)
    )
    for z in range(Z):
        first = jnp.min(ids_own[Z + z : Z + z + 1, :], axis=1, keepdims=True)
        before = jnp.where(last_ref[...] < first, 1.0 / ROWS, 0.0)
        lo_ref[z] = jnp.sum(before).astype(jnp.int32)

    def scores(q4, p):
        return lax.dot_general(
            q4, k_buf[p], (((1,), (1,)), ((), ())), preferred_element_type=jnp.float32
        )

    def weigh(slot, p):
        part = s_ref[slot]
        peak = jnp.concatenate([m_ref[...]] * 2, axis=1)
        weights = jnp.exp2((part - peak) * EXP2_SCALE).astype(jnp.bfloat16)
        return jnp.dot(weights, v_buf[p], preferred_element_type=jnp.float32)

    @pl.loop(0, Z)
    def _(z):
        q = q_ref[z]
        q4 = jnp.concatenate([q[:, g * HEAD_DIM : (g + 1) * HEAD_DIM] for g in range(GROUP)], axis=0)
        diag = Z + z
        count = jnp.clip(diag - lo_ref[z], 0, Z)
        steps = (count + 1) // 2
        qid = jnp.transpose(jnp.broadcast_to(ids_own[pl.ds(diag, 1), :], (ROWS, ROWS)))

        def put(slot, part, keep_own, keep_oth, start):
            for g in range(GROUP):
                rows = slice(g * ROWS, (g + 1) * ROWS)
                left = jnp.where(keep_own, part[rows, 0:ROWS], MASKED)
                right = jnp.where(keep_oth, part[rows, ROWS : 2 * ROWS], MASKED)
                s_ref[slot, rows, 0:ROWS] = left
                s_ref[slot, rows, ROWS : 2 * ROWS] = right
                most = jnp.maximum(left, right)
                m_ref[rows, :] = most if start else jnp.maximum(m_ref[rows, :], most)

        at_row = lax.broadcasted_iota(jnp.int32, (ROWS, ROWS), 0)
        at_col = lax.broadcasted_iota(jnp.int32, (ROWS, ROWS), 1)
        same_own = ids_own[pl.ds(diag, 1), :] == qid
        same_oth = ids_oth[pl.ds(diag, 1), :] == qid
        put(Z, scores(q4, diag), same_own & (at_col <= at_row), same_oth & odd, True)

        @pl.loop(0, steps)
        def _(k):
            for u in range(2):
                slot = 2 * k + u
                p = jnp.maximum(diag - 1 - slot, 0)
                put(
                    slot,
                    scores(q4, p),
                    ids_own[pl.ds(p, 1), :] == qid,
                    ids_oth[pl.ds(p, 1), :] == qid,
                    False,
                )

        m_ref[...] = jnp.broadcast_to(
            jnp.max(m_ref[...], axis=1, keepdims=True), (GROUP * ROWS, ROWS)
        )
        acc_ref[...] = weigh(Z, diag)

        @pl.loop(0, steps)
        def _(k):
            total = None
            for u in range(2):
                slot = 2 * k + u
                p = jnp.maximum(diag - 1 - slot, 0)
                term = weigh(slot, p)
                total = term if total is None else total + term
            acc_ref[...] += total

        for g in range(GROUP):
            rows = slice(g * ROWS, (g + 1) * ROWS)
            out = acc_ref[rows, 0:HEAD_DIM] / acc_ref[rows, HEAD_DIM : 2 * HEAD_DIM]
            o_ref[4 * z + 2 * (g % 2) + g // 2] = out.astype(jnp.bfloat16)


def pick_kernel(w_ref, two_ref, three_ref):
    z_here = 2 * lax.axis_index("zh") + lax.axis_index("zl")
    for k in range(Z - 3):
        ref, at = (two_ref, k) if k < 2 else (three_ref, k - 2)
        ref[at] = w_ref[lax.rem(z_here + 2 + k, Z)]


def projection_kernel(spread_ref, *refs):
    w_refs, (keep_ref, send_ref, other_ref, a_buf) = refs[:-4], refs[-4:]
    step, steps = pl.program_id(0), pl.num_programs(0)
    x = lax.axis_index("x")

    @pl.when(step == 0)
    def _():
        core = lax.axis_index("core")
        yl = lax.axis_index("yl")
        z_here = 2 * lax.axis_index("zh") + lax.axis_index("zl")
        for t in range(2):
            for u in range(2):
                source = 2 * (core if t == 0 else 1 - core) + (yl if u == 0 else 1 - yl)
                at = (2 * t + u) * ROWS
                for k, shift in enumerate(Z_ORDER):
                    z = lax.rem(z_here + shift, Z)
                    a_buf[at : at + ROWS, k * ROWS : (k + 1) * ROWS] = spread_ref[4 * z + source]

    piece = w_refs[0].shape[-1]
    for n, shift in enumerate((0, 3, 1, 2)):
        y, at = None, 0
        for part in w_refs[3 * n : 3 * n + 3]:
            depth = part.shape[0] * ROWS
            w = part[...].reshape(depth, piece)
            term = jnp.dot(a_buf[:, at : at + depth], w, preferred_element_type=jnp.float32)
            y, at = (term if y is None else y + term), at + depth
        y = y.astype(jnp.bfloat16)
        block = lax.rem(x + shift, 4) * steps + step
        cols = pl.ds(pl.multiple_of(block * piece, piece), piece)
        keep_ref[:, cols] = y[0:ROWS]
        send_ref[:, cols] = y[ROWS : 2 * ROWS]
        for u in range(2):
            other_ref[u, :, cols] = y[(2 + u) * ROWS : (3 + u) * ROWS]


def finish_kernel(keep_ref, arrived_ref, last_ref, o_ref):
    total = keep_ref[...].astype(jnp.float32) + arrived_ref[0].astype(jnp.float32)
    o_ref[...] = (total + last_ref[...].astype(jnp.float32)).astype(jnp.bfloat16)


def body(queries, keys, values, doc_ids, out_weight):
    bf16 = jnp.bfloat16
    def params(mib):
        return pltpu.CompilerParams(vmem_limit_bytes=mib * MIB)

    core = lax.axis_index("core")
    out_cols = out_weight.shape[1]
    swap = [(0, 1), (1, 0)]

    packed = pl.pallas_call(
        pack_kernel,
        out_shape=jax.ShapeDtypeStruct((Z, ROWS + 16, 2 * HEAD_DIM), bf16),
        compiler_params=params(8),
        name="pack_kv",
    )(keys, values, doc_ids.reshape(1, ROWS))
    def ring(axis, size, step):
        return lambda a: lax.ppermute(a, axis, [(i, (i + step) % size) for i in range(size)])

    x_up, x_down = ring("x", 4, 1), ring("x", 4, -1)

    piece = lax.dynamic_slice(
        out_weight, (core * ROWS, lax.axis_index("x") * (out_cols // 4)), (ROWS, out_cols // 4)
    )
    piece = lax.ppermute(piece, ("yl", "yh"), [(0, 0), (1, 2), (2, 1), (3, 3)])
    piece, packed = lax.optimization_barrier((piece, packed))
    own = lax.all_to_all(packed, ("zh", "zl"), 0, 0, tiled=True)
    here = lax.all_gather(piece, ("zh", "zl"), axis=0, tiled=False)
    up1 = ring(("zh", "zl"), Z, 1)(piece)
    down1 = ring(("zh", "zl"), Z, -1)(piece)

    own = lax.all_to_all(packed, ("zh", "zl"), 0, 0, tiled=True)
    own, up1, down1 = lax.optimization_barrier((own, up1, down1))
    group1 = jnp.stack([piece, up1, down1])
    before1, after1 = x_up(group1), x_down(group1)
    far1 = x_up(before1)
    other = lax.ppermute(own, "yh", swap)
    prev_own = lax.ppermute(own, BLK, [(i, i + 1) for i in range(15)])
    prev_other_0 = lax.ppermute(
        own,
        BLK + ("yh",),
        [(2 * i + h, 2 * (i + 1) + 1 - h) for i in range(1, 15, 2) for h in range(2)],
    )
    prev_other_1 = lax.ppermute(other, "core", [(0, 1)])

    split = queries.reshape(ROWS, Z, GROUP * HEAD_DIM).transpose(1, 0, 2)
    query = lax.all_to_all(split, ("zh", "zl"), 0, 0, tiled=True)
    query, here, far1, after1 = lax.optimization_barrier((query, here, far1, after1))
    group2, group3 = pl.pallas_call(
        pick_kernel,
        out_shape=[jax.ShapeDtypeStruct((n, ROWS, out_cols // 4), bf16) for n in (2, 3)],
        compiler_params=params(16),
        name="pick",
    )(here)
    before2, after2 = x_up(group2), x_down(group2)
    before3, after3 = x_up(group3), x_down(group3)
    attn = pl.pallas_call(
        attention_kernel,
        out_shape=jax.ShapeDtypeStruct((4 * Z, ROWS, HEAD_DIM), bf16),
        scratch_shapes=[
            pltpu.VMEM((PAIRS, 2 * ROWS, HEAD_DIM), bf16),
            pltpu.VMEM((PAIRS, 2 * ROWS, 2 * HEAD_DIM), bf16),
            pltpu.VMEM((PAIRS, ROWS), jnp.float32),
            pltpu.VMEM((PAIRS, ROWS), jnp.float32),
            pltpu.VMEM((PAIRS, ROWS), jnp.float32),
            pltpu.SMEM((Z,), jnp.int32),
            pltpu.VMEM((Z + 1, GROUP * ROWS, 2 * ROWS), jnp.float32),
            pltpu.VMEM((GROUP * ROWS, ROWS), jnp.float32),
            pltpu.VMEM((GROUP * ROWS, 2 * HEAD_DIM), jnp.float32),
        ],
        compiler_params=params(24),
        cost_estimate=pl.CostEstimate(
            flops=16_000_000_000, bytes_accessed=6_000_000, transcendentals=4_000_000
        ),
        name="attention",
    )(query, own, other, prev_own, prev_other_0, prev_other_1)

    attn, before2, after3 = lax.optimization_barrier((attn, before2, after3))
    spread = lax.all_to_all(attn, ("zh", "zl", "core", "yl"), 0, 0, tiled=True)
    far2, far3 = x_up(before2), x_down(after3)
    weights = (
        group1, group2, group3, before1, before2, before3, after1, after2, after3, far1, far2, far3
    )
    f32 = jnp.float32
    one = jax.ShapeDtypeStruct((ROWS, out_cols), bf16)
    steps = 4
    whole = pl.BlockSpec(memory_space=pltpu.VMEM)
    keep, send, theirs = pl.pallas_call(
        projection_kernel,
        grid=(steps,),
        in_specs=[whole]
        + [
            pl.BlockSpec((w.shape[0], ROWS, out_cols // 4 // steps), lambda i: (0, 0, i))
            for w in weights
        ],
        out_specs=[whole] * 3,
        out_shape=[one, one, jax.ShapeDtypeStruct((2, ROWS, out_cols), bf16)],
        scratch_shapes=[pltpu.VMEM((4 * ROWS, Z * ROWS), bf16)],
        compiler_params=params(54),
        cost_estimate=pl.CostEstimate(
            flops=2 * 4 * ROWS * Z * ROWS * out_cols,
            bytes_accessed=2 * Z * ROWS * out_cols + 8 * ROWS * out_cols,
            transcendentals=0,
        ),
        name="projection",
    )(spread, *weights)
    arrived = lax.ppermute(theirs, "core", swap)
    last = lax.ppermute((send.astype(f32) + arrived[1].astype(f32)).astype(bf16), "yl", swap)
    return pl.pallas_call(
        finish_kernel,
        out_shape=one,
        compiler_params=params(16),
        name="finish",
    )(keep, arrived, last)


def solution(mesh):
    torus = Mesh(mesh.devices.reshape(4, 2, 2, 4, 2, 2), AXES)
    uly = ("zh", "zl", "yh")
    rows = P(BLK + uly, None)
    in_specs = (rows, rows, rows, P(BLK + uly), P(uly, None))
    return jax.shard_map(body, mesh=torus, in_specs=in_specs, out_specs=rows, check_vma=False)
```

```python
import functools
import math

import jax
import jax.numpy as jnp
from jax import lax
from jax.experimental import pallas as pl
from jax.experimental.pallas import tpu as pltpu
from jax.sharding import Mesh
from jax.sharding import PartitionSpec as P

HEAD_DIM = 128
ROWS = 128
Z = 8
GROUP = 4
PAIRS = 16
EXP2_SCALE = math.log2(math.e) / math.sqrt(HEAD_DIM)
MASKED = -1e30
MIB = 1024 * 1024

AXES = ("x", "yl", "core", "zh", "zl", "yh")
BLK = ("x", "yl", "core")


def pack_kernel(k_ref, v_ref, id_ref, o_ref):
    ids = jnp.broadcast_to((id_ref[...] + 1).astype(jnp.float32), (16, ROWS)).astype(jnp.bfloat16)
    for g in range(Z):
        cols = slice(g * HEAD_DIM, (g + 1) * HEAD_DIM)
        o_ref[g, 0:ROWS, 0:HEAD_DIM] = k_ref[:, cols]
        o_ref[g, 0:ROWS, HEAD_DIM : 2 * HEAD_DIM] = v_ref[:, cols]
        o_ref[g, ROWS : ROWS + 16, 0:HEAD_DIM] = ids
        o_ref[g, ROWS : ROWS + 16, HEAD_DIM : 2 * HEAD_DIM] = ids


def attention_kernel(
    q_ref, own_ref, oth_ref, pown_ref, poth0_ref, poth1_ref, o_ref,
    k_buf, v_buf, ids_own, ids_oth, last_ref, lo_ref, s_ref, m_ref, acc_ref,
):
    odd = lax.axis_index("yh") == 1
    ones = jnp.ones((2 * ROWS, HEAD_DIM), jnp.bfloat16)
    for side, (a, b) in enumerate((((pown_ref,), (poth0_ref, poth1_ref)), ((own_ref,), (oth_ref,)))):
        for g in range(Z):
            p = side * Z + g
            for half, parts in enumerate((a, b)):
                block = parts[0][g] if len(parts) == 1 else parts[0][g] + parts[1][g]
                rows = slice(half * ROWS, (half + 1) * ROWS)
                k_buf[p, rows, :] = block[0:ROWS, 0:HEAD_DIM]
                v_buf[p, rows, 0:HEAD_DIM] = block[0:ROWS, HEAD_DIM : 2 * HEAD_DIM]
                ids = block[ROWS : ROWS + 16, 0:HEAD_DIM].astype(jnp.float32)[0:1, :]
                (ids_own if half == 0 else ids_oth)[p : p + 1, :] = ids
            v_buf[p, :, HEAD_DIM : 2 * HEAD_DIM] = ones
    last_ref[...] = jnp.broadcast_to(
        jnp.max(jnp.maximum(ids_own[...], ids_oth[...]), axis=1, keepdims=True), (PAIRS, ROWS)
    )
    for z in range(Z):
        first = jnp.min(ids_own[Z + z : Z + z + 1, :], axis=1, keepdims=True)
        before = jnp.where(last_ref[...] < first, 1.0 / ROWS, 0.0)
        lo_ref[z] = jnp.sum(before).astype(jnp.int32)

    def scores(q4, p):
        return lax.dot_general(
            q4, k_buf[p], (((1,), (1,)), ((), ())), preferred_element_type=jnp.float32
        )

    def weigh(slot, p):
        part = s_ref[slot]
        peak = jnp.concatenate([m_ref[...]] * 2, axis=1)
        weights = jnp.exp2((part - peak) * EXP2_SCALE).astype(jnp.bfloat16)
        return jnp.dot(weights, v_buf[p], preferred_element_type=jnp.float32)

    @pl.loop(0, Z)
    def _(z):
        q = q_ref[z]
        q4 = jnp.concatenate([q[:, g * HEAD_DIM : (g + 1) * HEAD_DIM] for g in range(GROUP)], axis=0)
        diag = Z + z
        count = jnp.clip(diag - lo_ref[z], 0, Z)
        steps = (count + 1) // 2
        qid = jnp.transpose(jnp.broadcast_to(ids_own[pl.ds(diag, 1), :], (ROWS, ROWS)))

        def put(slot, part, keep_own, keep_oth, start):
            for g in range(GROUP):
                rows = slice(g * ROWS, (g + 1) * ROWS)
                left = jnp.where(keep_own, part[rows, 0:ROWS], MASKED)
                right = jnp.where(keep_oth, part[rows, ROWS : 2 * ROWS], MASKED)
                s_ref[slot, rows, 0:ROWS] = left
                s_ref[slot, rows, ROWS : 2 * ROWS] = right
                most = jnp.maximum(left, right)
                m_ref[rows, :] = most if start else jnp.maximum(m_ref[rows, :], most)

        at_row = lax.broadcasted_iota(jnp.int32, (ROWS, ROWS), 0)
        at_col = lax.broadcasted_iota(jnp.int32, (ROWS, ROWS), 1)
        same_own = ids_own[pl.ds(diag, 1), :] == qid
        same_oth = ids_oth[pl.ds(diag, 1), :] == qid
        put(Z, scores(q4, diag), same_own & (at_col <= at_row), same_oth & odd, True)

        @pl.loop(0, steps)
        def _(k):
            for u in range(2):
                slot = 2 * k + u
                p = jnp.maximum(diag - 1 - slot, 0)
                put(
                    slot,
                    scores(q4, p),
                    ids_own[pl.ds(p, 1), :] == qid,
                    ids_oth[pl.ds(p, 1), :] == qid,
                    False,
                )

        m_ref[...] = jnp.broadcast_to(
            jnp.max(m_ref[...], axis=1, keepdims=True), (GROUP * ROWS, ROWS)
        )
        acc_ref[...] = weigh(Z, diag)

        @pl.loop(0, steps)
        def _(k):
            total = None
            for u in range(2):
                slot = 2 * k + u
                p = jnp.maximum(diag - 1 - slot, 0)
                term = weigh(slot, p)
                total = term if total is None else total + term
            acc_ref[...] += total

        for g in range(GROUP):
            rows = slice(g * ROWS, (g + 1) * ROWS)
            out = acc_ref[rows, 0:HEAD_DIM] / acc_ref[rows, HEAD_DIM : 2 * HEAD_DIM]
            o_ref[4 * z + 2 * (g % 2) + g // 2] = out.astype(jnp.bfloat16)


def projection_kernel(spread_ref, *refs):
    w_refs, (keep_ref, send_ref, other_ref, a_buf) = refs[:-4], refs[-4:]
    core = lax.axis_index("core")
    yl = lax.axis_index("yl")
    for t in range(2):
        for u in range(2):
            source = 2 * (core if t == 0 else 1 - core) + (yl if u == 0 else 1 - yl)
            at = (2 * t + u) * ROWS
            for z in range(Z):
                a_buf[at : at + ROWS, z * ROWS : (z + 1) * ROWS] = spread_ref[4 * z + source]
    at = 0
    for ref in w_refs:
        y, done = None, 0
        for part in ref if isinstance(ref, tuple) else (ref,):
            depth = part.shape[0] * ROWS
            term = jnp.dot(
                a_buf[:, done : done + depth],
                part[...].reshape(depth, part.shape[-1]),
                preferred_element_type=jnp.float32,
            )
            y, done = (term if y is None else y + term), done + depth
        y = y.astype(jnp.bfloat16)
        cols = slice(at, at + y.shape[1])
        at += y.shape[1]
        keep_ref[:, cols] = y[0:ROWS]
        send_ref[:, cols] = y[ROWS : 2 * ROWS]
        for u in range(2):
            other_ref[u, :, cols] = y[(2 + u) * ROWS : (3 + u) * ROWS]


def far_kernel(spread_ref, *refs):
    projection_kernel(spread_ref, refs[:2], *refs[2:])


def finish_kernel(*refs):
    o_ref = refs[-1]
    piece = o_ref.shape[-1] // 4
    x = lax.axis_index("x")
    for n, shift in enumerate((0, 3, 1, 2)):
        keep, arrived, last = refs[0:3] if n < 3 else refs[3:6]
        cols = slice((n % 3) * piece, (n % 3 + 1) * piece)
        total = keep[:, cols].astype(jnp.float32) + arrived[0, :, cols].astype(jnp.float32)
        total = total + last[:, cols].astype(jnp.float32)
        at = pl.multiple_of(lax.rem(x + shift, 4) * piece, piece)
        o_ref[:, pl.ds(at, piece)] = total.astype(jnp.bfloat16)


def body(queries, keys, values, doc_ids, out_weight):
    bf16 = jnp.bfloat16
    def params(mib):
        return pltpu.CompilerParams(vmem_limit_bytes=mib * MIB)

    core = lax.axis_index("core")
    out_cols = out_weight.shape[1]
    swap = [(0, 1), (1, 0)]

    packed = pl.pallas_call(
        pack_kernel,
        out_shape=jax.ShapeDtypeStruct((Z, ROWS + 16, 2 * HEAD_DIM), bf16),
        compiler_params=params(8),
        name="pack_kv",
    )(keys, values, doc_ids.reshape(1, ROWS))
    def ring(axis, size, step):
        return lambda a: lax.ppermute(a, axis, [(i, (i + step) % size) for i in range(size)])

    x_up, x_down = ring("x", 4, 1), ring("x", 4, -1)

    piece = lax.dynamic_slice(
        out_weight, (core * ROWS, lax.axis_index("x") * (out_cols // 4)), (ROWS, out_cols // 4)
    )
    piece = lax.ppermute(piece, ("yl", "yh"), [(0, 0), (1, 2), (2, 1), (3, 3)])
    piece, packed = lax.optimization_barrier((piece, packed))
    own = lax.all_to_all(packed, ("zh", "zl"), 0, 0, tiled=True)
    here = lax.all_gather(piece, ("zh", "zl"), axis=0, tiled=False)
    other = lax.ppermute(own, "yh", swap)
    prev_own = lax.ppermute(own, BLK, [(i, i + 1) for i in range(15)])
    prev_other_0 = lax.ppermute(
        own,
        BLK + ("yh",),
        [(2 * i + h, 2 * (i + 1) + 1 - h) for i in range(1, 15, 2) for h in range(2)],
    )
    prev_other_1 = lax.ppermute(other, "core", [(0, 1)])

    split = queries.reshape(ROWS, Z, GROUP * HEAD_DIM).transpose(1, 0, 2)
    query = lax.all_to_all(split, ("zh", "zl"), 0, 0, tiled=True)
    query, here = lax.optimization_barrier((query, here))
    before, after = x_up(here), x_down(here)
    attn = pl.pallas_call(
        attention_kernel,
        out_shape=jax.ShapeDtypeStruct((4 * Z, ROWS, HEAD_DIM), bf16),
        scratch_shapes=[
            pltpu.VMEM((PAIRS, 2 * ROWS, HEAD_DIM), bf16),
            pltpu.VMEM((PAIRS, 2 * ROWS, 2 * HEAD_DIM), bf16),
            pltpu.VMEM((PAIRS, ROWS), jnp.float32),
            pltpu.VMEM((PAIRS, ROWS), jnp.float32),
            pltpu.VMEM((PAIRS, ROWS), jnp.float32),
            pltpu.SMEM((Z,), jnp.int32),
            pltpu.VMEM((Z + 1, GROUP * ROWS, 2 * ROWS), jnp.float32),
            pltpu.VMEM((GROUP * ROWS, ROWS), jnp.float32),
            pltpu.VMEM((GROUP * ROWS, 2 * HEAD_DIM), jnp.float32),
        ],
        compiler_params=params(24),
        cost_estimate=pl.CostEstimate(
            flops=16_000_000_000, bytes_accessed=6_000_000, transcendentals=4_000_000
        ),
        name="attention",
    )(query, own, other, prev_own, prev_other_0, prev_other_1)

    spread = lax.all_to_all(attn, ("zh", "zl", "core", "yl"), 0, 0, tiled=True)
    far = x_up(before[: Z // 2]), x_down(after[Z // 2 :])
    f32 = jnp.float32
    parts = []
    for kernel, weights, blocks in (
        (projection_kernel, (here, before, after), 3),
        (far_kernel, far, 1),
    ):
        cols = blocks * out_cols // 4
        if parts:
            parts[2] = lax.ppermute(parts[2], "yl", swap)
            spread, parts[2] = lax.optimization_barrier((spread, parts[2]))
        one = jax.ShapeDtypeStruct((ROWS, cols), bf16)
        keep, send, theirs = pl.pallas_call(
            kernel,
            out_shape=[one, one, jax.ShapeDtypeStruct((2, ROWS, cols), bf16)],
            scratch_shapes=[pltpu.VMEM((4 * ROWS, Z * ROWS), bf16)],
            compiler_params=params(40),
            cost_estimate=pl.CostEstimate(
                flops=2 * 4 * ROWS * Z * ROWS * cols,
                bytes_accessed=2 * Z * ROWS * cols + 8 * ROWS * cols,
                transcendentals=0,
            ),
            name="projection",
        )(spread, *weights)
        arrived = lax.ppermute(theirs, "core", swap)
        parts += [keep, arrived, (send.astype(f32) + arrived[1].astype(f32)).astype(bf16)]
    parts[5] = lax.ppermute(parts[5], "yl", swap)
    return pl.pallas_call(
        finish_kernel,
        out_shape=jax.ShapeDtypeStruct((ROWS, out_cols), bf16),
        compiler_params=params(16),
        name="finish",
    )(*parts)


def solution(mesh):
    torus = Mesh(mesh.devices.reshape(4, 2, 2, 4, 2, 2), AXES)
    uly = ("zh", "zl", "yh")
    rows = P(BLK + uly, None)
    in_specs = (rows, rows, rows, P(BLK + uly), P(uly, None))
    return jax.shard_map(body, mesh=torus, in_specs=in_specs, out_specs=rows, check_vma=False)
```

```python
import functools
import math

import jax
import jax.numpy as jnp
from jax import lax
from jax.experimental import pallas as pl
from jax.experimental.pallas import tpu as pltpu
from jax.sharding import Mesh
from jax.sharding import PartitionSpec as P

HEAD_DIM = 128
ROWS = 128
Z = 8
GROUP = 4
PAIRS = 16
EXP2_SCALE = math.log2(math.e) / math.sqrt(HEAD_DIM)
MASKED = -1e30
MIB = 1024 * 1024

AXES = ("x", "yl", "core", "zh", "zl", "yh")
BLK = ("x", "yl", "core")


def pack_kernel(k_ref, v_ref, id_ref, o_ref):
    ids = jnp.broadcast_to((id_ref[...] + 1).astype(jnp.float32), (16, ROWS)).astype(jnp.bfloat16)
    for g in range(Z):
        cols = slice(g * HEAD_DIM, (g + 1) * HEAD_DIM)
        o_ref[g, 0:ROWS, 0:HEAD_DIM] = k_ref[:, cols]
        o_ref[g, 0:ROWS, HEAD_DIM : 2 * HEAD_DIM] = v_ref[:, cols]
        o_ref[g, ROWS : ROWS + 16, 0:HEAD_DIM] = ids
        o_ref[g, ROWS : ROWS + 16, HEAD_DIM : 2 * HEAD_DIM] = ids


def attention_kernel(
    q_ref, own_ref, oth_ref, pown_ref, poth0_ref, poth1_ref, o_ref,
    k_buf, v_buf, ids_own, ids_oth, last_ref, lo_ref, s_ref, m_ref, acc_ref,
):
    odd = lax.axis_index("yh") == 1
    ones = jnp.ones((2 * ROWS, HEAD_DIM), jnp.bfloat16)
    for side, (a, b) in enumerate((((pown_ref,), (poth0_ref, poth1_ref)), ((own_ref,), (oth_ref,)))):
        for g in range(Z):
            p = side * Z + g
            for half, parts in enumerate((a, b)):
                block = parts[0][g] if len(parts) == 1 else parts[0][g] + parts[1][g]
                rows = slice(half * ROWS, (half + 1) * ROWS)
                k_buf[p, rows, :] = block[0:ROWS, 0:HEAD_DIM]
                v_buf[p, rows, 0:HEAD_DIM] = block[0:ROWS, HEAD_DIM : 2 * HEAD_DIM]
                ids = block[ROWS : ROWS + 16, 0:HEAD_DIM].astype(jnp.float32)[0:1, :]
                (ids_own if half == 0 else ids_oth)[p : p + 1, :] = ids
            v_buf[p, :, HEAD_DIM : 2 * HEAD_DIM] = ones
    last_ref[...] = jnp.broadcast_to(
        jnp.max(jnp.maximum(ids_own[...], ids_oth[...]), axis=1, keepdims=True), (PAIRS, ROWS)
    )
    for z in range(Z):
        first = jnp.min(ids_own[Z + z : Z + z + 1, :], axis=1, keepdims=True)
        before = jnp.where(last_ref[...] < first, 1.0 / ROWS, 0.0)
        lo_ref[z] = jnp.sum(before).astype(jnp.int32)

    def scores(q4, p):
        return lax.dot_general(
            q4, k_buf[p], (((1,), (1,)), ((), ())), preferred_element_type=jnp.float32
        )

    def weigh(slot, p):
        part = s_ref[slot]
        peak = jnp.concatenate([m_ref[...]] * 2, axis=1)
        weights = jnp.exp2((part - peak) * EXP2_SCALE).astype(jnp.bfloat16)
        return jnp.dot(weights, v_buf[p], preferred_element_type=jnp.float32)

    @pl.loop(0, Z)
    def _(z):
        q = q_ref[z]
        q4 = jnp.concatenate([q[:, g * HEAD_DIM : (g + 1) * HEAD_DIM] for g in range(GROUP)], axis=0)
        diag = Z + z
        count = jnp.clip(diag - lo_ref[z], 0, Z)
        steps = (count + 1) // 2
        qid = jnp.transpose(jnp.broadcast_to(ids_own[pl.ds(diag, 1), :], (ROWS, ROWS)))

        def put(slot, part, keep_own, keep_oth, start):
            for g in range(GROUP):
                rows = slice(g * ROWS, (g + 1) * ROWS)
                left = jnp.where(keep_own, part[rows, 0:ROWS], MASKED)
                right = jnp.where(keep_oth, part[rows, ROWS : 2 * ROWS], MASKED)
                s_ref[slot, rows, 0:ROWS] = left
                s_ref[slot, rows, ROWS : 2 * ROWS] = right
                most = jnp.maximum(left, right)
                m_ref[rows, :] = most if start else jnp.maximum(m_ref[rows, :], most)

        at_row = lax.broadcasted_iota(jnp.int32, (ROWS, ROWS), 0)
        at_col = lax.broadcasted_iota(jnp.int32, (ROWS, ROWS), 1)
        same_own = ids_own[pl.ds(diag, 1), :] == qid
        same_oth = ids_oth[pl.ds(diag, 1), :] == qid
        put(Z, scores(q4, diag), same_own & (at_col <= at_row), same_oth & odd, True)

        @pl.loop(0, steps)
        def _(k):
            for u in range(2):
                slot = 2 * k + u
                p = jnp.maximum(diag - 1 - slot, 0)
                put(
                    slot,
                    scores(q4, p),
                    ids_own[pl.ds(p, 1), :] == qid,
                    ids_oth[pl.ds(p, 1), :] == qid,
                    False,
                )

        m_ref[...] = jnp.broadcast_to(
            jnp.max(m_ref[...], axis=1, keepdims=True), (GROUP * ROWS, ROWS)
        )
        acc_ref[...] = weigh(Z, diag)

        @pl.loop(0, steps)
        def _(k):
            total = None
            for u in range(2):
                slot = 2 * k + u
                p = jnp.maximum(diag - 1 - slot, 0)
                term = weigh(slot, p)
                total = term if total is None else total + term
            acc_ref[...] += total

        for g in range(GROUP):
            rows = slice(g * ROWS, (g + 1) * ROWS)
            out = acc_ref[rows, 0:HEAD_DIM] / acc_ref[rows, HEAD_DIM : 2 * HEAD_DIM]
            o_ref[4 * z + 2 * (g % 2) + g // 2] = out.astype(jnp.bfloat16)


def projection_kernel(spread_ref, *refs):
    w_refs, (keep_ref, send_ref, other_ref, a_buf) = refs[:-4], refs[-4:]
    core = lax.axis_index("core")
    yl = lax.axis_index("yl")
    for t in range(2):
        for u in range(2):
            source = 2 * (core if t == 0 else 1 - core) + (yl if u == 0 else 1 - yl)
            at = (2 * t + u) * ROWS
            for z in range(Z):
                a_buf[at : at + ROWS, z * ROWS : (z + 1) * ROWS] = spread_ref[4 * z + source]
    at = 0
    for ref in w_refs:
        y, done = None, 0
        for part in ref if isinstance(ref, tuple) else (ref,):
            depth = part.shape[0] * ROWS
            term = jnp.dot(
                a_buf[:, done : done + depth],
                part[...].reshape(depth, part.shape[-1]),
                preferred_element_type=jnp.float32,
            )
            y, done = (term if y is None else y + term), done + depth
        y = y.astype(jnp.bfloat16)
        cols = slice(at, at + y.shape[1])
        at += y.shape[1]
        keep_ref[:, cols] = y[0:ROWS]
        send_ref[:, cols] = y[ROWS : 2 * ROWS]
        for u in range(2):
            other_ref[u, :, cols] = y[(2 + u) * ROWS : (3 + u) * ROWS]


def far_kernel(spread_ref, *refs):
    projection_kernel(spread_ref, refs[:2], *refs[2:])


def finish_kernel(*refs):
    o_ref = refs[-1]
    piece = o_ref.shape[-1] // 4
    x = lax.axis_index("x")
    for n, shift in enumerate((0, 3, 1, 2)):
        keep, arrived, last = refs[0:3] if n < 3 else refs[3:6]
        cols = slice((n % 3) * piece, (n % 3 + 1) * piece)
        total = keep[:, cols].astype(jnp.float32) + arrived[0, :, cols].astype(jnp.float32)
        total = total + last[:, cols].astype(jnp.float32)
        at = pl.multiple_of(lax.rem(x + shift, 4) * piece, piece)
        o_ref[:, pl.ds(at, piece)] = total.astype(jnp.bfloat16)


def body(queries, keys, values, doc_ids, out_weight):
    bf16 = jnp.bfloat16
    def params(mib):
        return pltpu.CompilerParams(vmem_limit_bytes=mib * MIB)

    core = lax.axis_index("core")
    out_cols = out_weight.shape[1]
    swap = [(0, 1), (1, 0)]

    packed = pl.pallas_call(
        pack_kernel,
        out_shape=jax.ShapeDtypeStruct((Z, ROWS + 16, 2 * HEAD_DIM), bf16),
        compiler_params=params(56),
        name="pack_kv",
    )(keys, values, doc_ids.reshape(1, ROWS))
    def ring(axis, size, step):
        return lambda a: lax.ppermute(a, axis, [(i, (i + step) % size) for i in range(size)])

    x_up, x_down = ring("x", 4, 1), ring("x", 4, -1)

    piece = lax.dynamic_slice(
        out_weight, (core * ROWS, lax.axis_index("x") * (out_cols // 4)), (ROWS, out_cols // 4)
    )
    piece = lax.ppermute(piece, ("yl", "yh"), [(0, 0), (1, 2), (2, 1), (3, 3)])
    piece, packed = lax.optimization_barrier((piece, packed))
    own = lax.all_to_all(packed, ("zh", "zl"), 0, 0, tiled=True)
    here = lax.all_gather(piece, ("zh", "zl"), axis=0, tiled=False)
    other = lax.ppermute(own, "yh", swap)
    prev_own = lax.ppermute(own, BLK, [(i, i + 1) for i in range(15)])
    prev_other_0 = lax.ppermute(
        own,
        BLK + ("yh",),
        [(2 * i + h, 2 * (i + 1) + 1 - h) for i in range(1, 15, 2) for h in range(2)],
    )
    prev_other_1 = lax.ppermute(other, "core", [(0, 1)])

    split = queries.reshape(ROWS, Z, GROUP * HEAD_DIM).transpose(1, 0, 2)
    query = lax.all_to_all(split, ("zh", "zl"), 0, 0, tiled=True)
    query, here = lax.optimization_barrier((query, here))
    before, after = x_up(here), x_down(here)
    attn = pl.pallas_call(
        attention_kernel,
        out_shape=jax.ShapeDtypeStruct((4 * Z, ROWS, HEAD_DIM), bf16),
        scratch_shapes=[
            pltpu.VMEM((PAIRS, 2 * ROWS, HEAD_DIM), bf16),
            pltpu.VMEM((PAIRS, 2 * ROWS, 2 * HEAD_DIM), bf16),
            pltpu.VMEM((PAIRS, ROWS), jnp.float32),
            pltpu.VMEM((PAIRS, ROWS), jnp.float32),
            pltpu.VMEM((PAIRS, ROWS), jnp.float32),
            pltpu.SMEM((Z,), jnp.int32),
            pltpu.VMEM((Z + 1, GROUP * ROWS, 2 * ROWS), jnp.float32),
            pltpu.VMEM((GROUP * ROWS, ROWS), jnp.float32),
            pltpu.VMEM((GROUP * ROWS, 2 * HEAD_DIM), jnp.float32),
        ],
        compiler_params=params(24),
        cost_estimate=pl.CostEstimate(
            flops=16_000_000_000, bytes_accessed=6_000_000, transcendentals=4_000_000
        ),
        name="attention",
    )(query, own, other, prev_own, prev_other_0, prev_other_1)

    spread = lax.all_to_all(attn, ("zh", "zl", "core", "yl"), 0, 0, tiled=True)
    far = x_up(before[: Z // 2]), x_down(after[Z // 2 :])
    f32 = jnp.float32
    parts = []
    for kernel, weights, blocks in (
        (projection_kernel, (here, before, after), 3),
        (far_kernel, far, 1),
    ):
        cols = blocks * out_cols // 4
        if parts:
            parts[2] = lax.ppermute(parts[2], "yl", swap)
            spread, parts[2] = lax.optimization_barrier((spread, parts[2]))
        one = jax.ShapeDtypeStruct((ROWS, cols), bf16)
        keep, send, theirs = pl.pallas_call(
            kernel,
            out_shape=[one, one, jax.ShapeDtypeStruct((2, ROWS, cols), bf16)],
            scratch_shapes=[pltpu.VMEM((4 * ROWS, Z * ROWS), bf16)],
            compiler_params=params(40),
            cost_estimate=pl.CostEstimate(
                flops=2 * 4 * ROWS * Z * ROWS * cols,
                bytes_accessed=2 * Z * ROWS * cols + 8 * ROWS * cols,
                transcendentals=0,
            ),
            name="projection",
        )(spread, *weights)
        arrived = lax.ppermute(theirs, "core", swap)
        parts += [keep, arrived, (send.astype(f32) + arrived[1].astype(f32)).astype(bf16)]
    parts[5] = lax.ppermute(parts[5], "yl", swap)
    return pl.pallas_call(
        finish_kernel,
        out_shape=jax.ShapeDtypeStruct((ROWS, out_cols), bf16),
        compiler_params=params(16),
        name="finish",
    )(*parts)


def solution(mesh):
    torus = Mesh(mesh.devices.reshape(4, 2, 2, 4, 2, 2), AXES)
    uly = ("zh", "zl", "yh")
    rows = P(BLK + uly, None)
    in_specs = (rows, rows, rows, P(BLK + uly), P(uly, None))
    return jax.shard_map(body, mesh=torus, in_specs=in_specs, out_specs=rows, check_vma=False)
```
